128 devices in a mesh: dp: 16 (over y, z), lib: 8 (over x, core).
Axes of the slice: x: 4, y: 4, z: 4, core: 2. Of those that a mesh axis runs over, the one named last changes fastest.
Arguments:
- hidden_in: bfloat16 [65536, 1024], P(('dp', 'lib')), may hold values from -40 to 40
- cotangent: bfloat16 [65536, 1024], P(('dp', 'lib')), may hold values from -1 to 1
- gains: float32 [1, 1024], replicated, may hold values from 0.1 to 1.9
- weights: bfloat16 [1, 4, 1024, 1024], replicated, may hold values from -0.125 to 0.125
- library: bfloat16 [2048, 128, 1024], P(('dp', 'lib')), may hold values from -96 to 96
- neighbours: int32 [1024, 2], P(('dp', 'lib')), may hold values from 0 to 127, as said below
- tile_home: int32 [16, 128], P('dp'), may hold values from 0 to 127, as said below
Outputs:
- hidden_out: bfloat16 [65536, 1024], P(('dp', 'lib'))
- input_grad: bfloat16 [65536, 1024], P(('dp', 'lib'))
- weight_grads: float32 [4096, 1024], P(('dp', 'lib'))
- gain_grads: float32 [1024], P(('dp', 'lib'))
The draws below stay inside these ranges and needn't reach their ends.
Inputs may be any that keep to these rules, and one draw needn't show every extreme that they name: `tile_home`: row g of each is a permutation of 0 to 127; storage row r of part g is library row g * 128 + r and lies on the device of dp index g and lib index r // 16. `neighbours`: rows are the query blocks of a device in order, 8 per device. Among the 16 ids of one device, at most 4 are stored on any one device of its dp index (owner = tile_home[g, id] // 16); in every draw, each dp index has one owner to which every device of that index sends exactly 4. Ids may repeat.
All inputs are finite; a program needn't handle non-finite values.
Results may differ from the reference program's by a relative error of at most 0.015.
The reference program's roundings to bfloat16 on the way count: a program that leaves them out, or rounds other values in their place, can miss the bound.
Values may be sent and summed in bfloat16 or wider, within the bound.
A program may use at most 128 MiB of HBM per device.

```python
import math
import jax
import jax.numpy as jnp
from jax import lax

D = 1024
HEADS = 16
HD = 64
LAYERS = 1
BLOCK = 64
BLOCKS_SEQ = 4
NEIGH = 2
TILE = 128
CAP = 4
LIB_DEV = 16
SEQ = 256
TOK_DEV = 512
BLOCKS_DEV = 8
REQ = 16
TOKENS = 65536
PART = 128
LIBRARY = 2048
N_DP = 16
N_LIB = 8


def routing(key):
    key = jax.random.fold_in(key, 5003)
    k_score, k_hot, k_order, k_slot, k_perm = jax.random.split(key, 5)
    n_cand = N_LIB * CAP
    n_spare = REQ - CAP
    pick_score = jax.random.randint(k_score, (N_DP, N_LIB, n_cand), 0, 1 << 16)
    hot_owner = jax.random.randint(k_hot, (N_DP, 1, 1), 0, N_LIB)
    cand_index = jnp.arange(n_cand, dtype=jnp.int32)[None, None, :]
    cand_owner = cand_index // CAP
    cand_score = pick_score * n_cand + cand_index + jnp.where(cand_owner == hot_owner, 1 << 30, 0)
    chosen = jnp.argsort(cand_score, axis=-1)[:, :, :n_spare] // CAP
    owners = jnp.concatenate([jnp.broadcast_to(hot_owner, (N_DP, N_LIB, CAP)), chosen], axis=-1)
    mix_score = jax.random.randint(k_order, (N_DP, N_LIB, REQ), 0, 1 << 16) * REQ + jnp.arange(REQ, dtype=jnp.int32)[None, None, :]
    owners = jnp.take_along_axis(owners, jnp.argsort(mix_score, axis=-1), axis=-1)
    slot_draw = jax.random.randint(k_slot, (N_DP, N_LIB, REQ), 0, LIB_DEV)
    stored = owners * LIB_DEV + slot_draw
    perm_score = jax.random.randint(k_perm, (N_DP, PART), 0, 1 << 16) * PART + jnp.arange(PART, dtype=jnp.int32)[None, :]
    home_rows = jnp.argsort(perm_score, axis=-1).astype(jnp.int32)
    where_is = jnp.argsort(home_rows, axis=-1).astype(jnp.int32)
    span_ids = jnp.take_along_axis(where_is, stored.reshape(N_DP, N_LIB * REQ), axis=1)
    return (span_ids.reshape(N_DP * N_LIB * BLOCKS_DEV, NEIGH).astype(jnp.int32), home_rows)


def draw_neighbours(key, part):
    span_ids, home_rows = routing(key)
    return span_ids


def draw_tile_home(key, part):
    span_ids, home_rows = routing(key)
    return home_rows


def draw_hidden_in(key, part):
    key = jax.random.fold_in(key, 11)
    k_row, k_col, k_val = jax.random.split(key, 3)
    row_scale = jnp.exp(jax.random.uniform(k_row, (TOKENS, 1), jnp.float32, math.log(0.3), math.log(3.0)))
    col_scale = jnp.exp(jax.random.uniform(k_col, (1, D), jnp.float32, math.log(0.3), math.log(3.0)))
    drawn = jax.random.truncated_normal(k_val, -4.0, 4.0, (TOKENS, D), jnp.float32) * row_scale * col_scale
    return drawn.astype(jnp.bfloat16)


def draw_library(key, part):
    key = jax.random.fold_in(key, 13)
    k_row, k_col, k_val = jax.random.split(key, 3)
    row_scale = jnp.exp(jax.random.uniform(k_row, (LIBRARY, TILE, 1), jnp.float32, math.log(0.3), math.log(3.0)))
    col_scale = jnp.exp(jax.random.uniform(k_col, (1, 1, D), jnp.float32, math.log(0.3), math.log(3.0)))
    drawn = jax.random.truncated_normal(k_val, -4.0, 4.0, (LIBRARY, TILE, D), jnp.float32) * row_scale * col_scale
    return drawn.astype(jnp.bfloat16)


def draw_weights(key, part):
    key = jax.random.fold_in(key, 17)
    fan_scale = D ** (-0.5)
    drawn = jax.random.truncated_normal(key, -4.0, 4.0, (LAYERS, 4, D, D), jnp.float32) * fan_scale
    return drawn.astype(jnp.bfloat16)


def draw_cotangent(key, part):
    key = jax.random.fold_in(key, 19)
    k_val = jax.random.fold_in(key, 0)
    drawn = jax.random.truncated_normal(k_val, -4.0, 4.0, (TOKENS, D), jnp.float32) * 0.25
    return drawn.astype(jnp.bfloat16)


def setup_inputs(seed: int = 0) -> dict:
    keys = jax.random.split(jax.random.key(seed), 8)
    return {
        "hidden_in": draw_hidden_in(jax.random.fold_in(keys[7], 71), 0),
        "cotangent": draw_cotangent(jax.random.fold_in(keys[7], 71), 0),
        "gains": jnp.clip(1.0 + 0.18 * jax.random.normal(keys[2], (LAYERS, D), jnp.float32), 0.1, 1.9),
        "weights": draw_weights(jax.random.fold_in(keys[7], 71), 0),
        "library": draw_library(jax.random.fold_in(keys[7], 71), 0),
        "neighbours": draw_neighbours(jax.random.fold_in(keys[7], 71), 0),
        "tile_home": draw_tile_home(jax.random.fold_in(keys[7], 71), 0),
    }


EPSILON = 1e-06

def matmul_f32(left, right):
    return jnp.dot(left, right, preferred_element_type=jnp.float32)

def batched_ref(form, left, right):
    return jnp.einsum(form, left.astype(jnp.float32), right.astype(jnp.float32), precision=lax.Precision.HIGHEST)

def shift_up(rows):
    n_seqs = rows.shape[0] // SEQ
    feat_dim = rows.shape[1]
    grouped = rows.reshape(n_seqs, SEQ, feat_dim)
    zero_pad = jnp.zeros((n_seqs, BLOCK - 1, feat_dim), rows.dtype)
    moved_rows = jnp.concatenate([grouped[:, BLOCK - 1:], zero_pad], axis=1)
    return moved_rows.reshape(n_seqs * BLOCKS_SEQ, BLOCK, feat_dim)

def shift_down(groups):
    feat_dim = groups.shape[-1]
    n_seqs = groups.shape[0] // BLOCKS_SEQ
    grouped = groups.reshape(n_seqs, SEQ, feat_dim)
    zero_pad = jnp.zeros((n_seqs, BLOCK - 1, feat_dim), groups.dtype)
    moved_rows = jnp.concatenate([zero_pad, grouped[:, :SEQ - BLOCK + 1]], axis=1)
    return moved_rows.reshape(n_seqs * SEQ, feat_dim)

def forward_layer(x_rows, gain_row, layer_w, tile_block, batched):
    n_blocks = tile_block.shape[0]
    feat_dim = x_rows.shape[1]
    x_float = x_rows.astype(jnp.float32)
    inv_rms = lax.rsqrt(lax.optimization_barrier(jnp.mean(x_float * x_float, axis=1, keepdims=True)) + EPSILON)
    normed = (x_float * inv_rms * gain_row[None, :]).astype(jnp.bfloat16)
    query = matmul_f32(normed, layer_w[0]).astype(jnp.bfloat16)
    tile_rows = tile_block.reshape(-1, feat_dim)
    key_rows = matmul_f32(tile_rows, layer_w[1]).astype(jnp.bfloat16).reshape(n_blocks, -1, HEADS, HD)
    values = matmul_f32(tile_rows, layer_w[2]).astype(jnp.bfloat16).reshape(n_blocks, -1, HEADS, HD)
    shifted = shift_up(query).reshape(n_blocks, BLOCK, HEADS, HD)
    scores = batched('cqhd,ckhd->chqk', shifted, key_rows) * HD ** (-0.5)
    row_max = lax.optimization_barrier(jnp.max(scores, axis=-1, keepdims=True))
    exp_scores = jnp.exp(scores - row_max)
    attn_prob = exp_scores / lax.optimization_barrier(jnp.sum(exp_scores, axis=-1, keepdims=True))
    prob_bf16 = attn_prob.astype(jnp.bfloat16)
    mixed_rows = batched('chqk,ckhd->cqhd', prob_bf16, values).astype(jnp.bfloat16)
    attn_out = shift_down(mixed_rows.reshape(n_blocks, BLOCK, feat_dim))
    layer_out = (x_float + matmul_f32(attn_out, layer_w[3])).astype(jnp.bfloat16)
    saved_state = (x_float, inv_rms, normed, shifted, key_rows, values, attn_prob, prob_bf16, attn_out)
    return (layer_out, saved_state)

def backward_layer(grad_flow, gain_row, layer_w, tile_block, saved_state, batched):
    x_float, inv_rms, normed, shifted, key_rows, values, attn_prob, prob_bf16, attn_out = saved_state
    n_blocks = tile_block.shape[0]
    feat_dim = x_float.shape[1]
    grad_bf16 = grad_flow.astype(jnp.bfloat16)
    d_wo = matmul_f32(attn_out.T, grad_bf16)
    d_attn = matmul_f32(grad_bf16, layer_w[3].T).astype(jnp.bfloat16)
    d_mixed = shift_up(d_attn).reshape(n_blocks, BLOCK, HEADS, HD)
    d_prob = batched('cqhd,ckhd->chqk', d_mixed, values)
    d_values = batched('chqk,cqhd->ckhd', prob_bf16, d_mixed).astype(jnp.bfloat16)
    row_dot = lax.optimization_barrier(jnp.sum(attn_prob * d_prob, axis=-1, keepdims=True))
    d_scores = (attn_prob * (d_prob - row_dot) * HD ** (-0.5)).astype(jnp.bfloat16)
    d_shifted = batched('chqk,ckhd->cqhd', d_scores, key_rows).astype(jnp.bfloat16)
    d_keys = batched('chqk,cqhd->ckhd', d_scores, shifted).astype(jnp.bfloat16)
    d_query = shift_down(d_shifted.reshape(n_blocks, BLOCK, feat_dim))
    tile_rows = tile_block.reshape(-1, feat_dim)
    d_wq = matmul_f32(normed.T, d_query)
    d_wk = matmul_f32(tile_rows.T, d_keys.reshape(-1, feat_dim))
    d_wv = matmul_f32(tile_rows.T, d_values.reshape(-1, feat_dim))
    d_normed = matmul_f32(d_query, layer_w[0].T)
    d_gain = lax.optimization_barrier(jnp.sum(d_normed * x_float * inv_rms, axis=0))
    d_hat = d_normed * gain_row[None, :]
    inner = lax.optimization_barrier(jnp.mean(d_hat * x_float, axis=1, keepdims=True))
    d_x = inv_rms * d_hat - x_float * (inv_rms * inv_rms * inv_rms) * inner
    return (grad_flow + d_x, jnp.stack([d_wq, d_wk, d_wv, d_wo]), d_gain)

def device_step(x_rows, cot_rows, gains, weights, tile_block, batched):
    current = x_rows
    saved_all = []
    for layer_idx in range(LAYERS):
        current, saved_state = forward_layer(current, gains[layer_idx], weights[layer_idx], tile_block, batched)
        saved_all.append(saved_state)
    grad_flow = cot_rows.astype(jnp.float32)
    w_parts = [None] * LAYERS
    g_parts = [None] * LAYERS
    for layer_idx in reversed(range(LAYERS)):
        grad_flow, w_parts[layer_idx], g_parts[layer_idx] = backward_layer(grad_flow, gains[layer_idx], weights[layer_idx], tile_block, saved_all[layer_idx], batched)
    return (current, grad_flow.astype(jnp.bfloat16), jnp.stack(w_parts), jnp.stack(g_parts))

def reference(hidden_in, cotangent, gains, weights, library, neighbours, tile_home):
    devices = N_DP * N_LIB
    tok_rows = hidden_in.reshape(devices, TOK_DEV, D)
    cot_rows = cotangent.reshape(devices, TOK_DEV, D)
    wanted = neighbours.reshape(devices, BLOCKS_DEV * NEIGH)

    def visit_device(running, device_item):
        w_sum, g_sum = running
        dev_index, x_rows, c_rows, asked_ids = device_item
        dp_row = (dev_index // N_LIB).astype(jnp.int32)
        home_row = lax.dynamic_index_in_dim(tile_home, dp_row, 0, keepdims=False)
        stored = jnp.take(home_row, asked_ids.astype(jnp.int32)).astype(jnp.int32)
        lib_rows = (dp_row * PART + stored).astype(jnp.int32)
        tile_block = jnp.take(library, lib_rows, axis=0).reshape(BLOCKS_DEV, NEIGH * TILE, D)
        out_part, grad_part, w_part, g_part = device_step(x_rows, c_rows, gains, weights, tile_block, batched_ref)
        return ((w_sum + w_part, g_sum + g_part), (out_part, grad_part))
    start_sums = (jnp.zeros((LAYERS, 4, D, D), jnp.float32), jnp.zeros((LAYERS, D), jnp.float32))
    (w_sum, g_sum), (out_rows, grad_rows) = lax.scan(visit_device, start_sums, (jnp.arange(devices, dtype=jnp.int32), tok_rows, cot_rows, wanted))
    return (out_rows.reshape(TOKENS, D), grad_rows.reshape(TOKENS, D), w_sum.reshape(LAYERS * 4 * D, D), g_sum.reshape(LAYERS * D))
```

```python
import functools

import jax
import jax.numpy as jnp
from jax import lax
from jax.experimental import pallas as pl
from jax.experimental.pallas import tpu as pltpu
from jax.sharding import PartitionSpec as P

HEADS = 16
HD = 64
BLOCK = 64
BLOCKS_SEQ = 4
CAP = 4
SEQ = 256
D = 1024
EPSILON = 1e-06

F32 = jnp.float32
BF16 = jnp.bfloat16
MESH = pl.DeviceIdType.MESH

PARTS = (
    (0, 384, ("x", "y", "z")),
    (384, 384, ("y", "z", "x")),
    (768, 256, ("z", "x", "y")),
)
DIMS = ("y", "z", "x")


def dot(left, right, dims=((1,), (0,))):
    return lax.dot_general(left, right, (dims, ((), ())), preferred_element_type=F32)


def my_coords():
    dp = lax.axis_index("dp")
    lib = lax.axis_index("lib")
    return {
        "y": lax.div(dp, 4),
        "z": lax.rem(dp, 4),
        "x": lax.div(lib, 2),
        "c": lax.rem(lib, 2),
    }


def device_of(at):
    return (at["y"] * 4 + at["z"], at["x"] * 2 + at["c"])


def along(me, axis, step):
    size = 2 if axis == "c" else 4
    return lax.rem(me[axis] + step, size)


def moved(me, axis, step):
    return device_of({**me, axis: along(me, axis, step)})


def stage_shapes(dims, width):
    rest = (4,) * (len(dims) - 1)
    chunk = rest + (32, width)
    half = ((2,) + rest[1:] + (32, width)) if rest else (16, width)
    return [half, half, chunk, chunk]


def part_scratch(part):
    _, width, order = part
    shapes = [pltpu.VMEM((2, 4, 4, 4, 32, width), BF16), pltpu.VMEM((4, 4, 4, 32, width), BF16)]
    dims = list(DIMS)
    n_copies = 1
    for pos, axis in enumerate(order):
        shapes += [pltpu.VMEM(s, BF16) for s in stage_shapes(dims, width)]
        n_copies += 4
        dims.remove(axis)
        if dims:
            shapes.append(pltpu.VMEM((4,) * len(dims) + (32, width), BF16))
    shapes += [pltpu.SemaphoreType.DMA((n_copies,)), pltpu.SemaphoreType.DMA((n_copies,))]
    return shapes


def reduce_part(me, part, bufs, w_out, sent):
    c0, width, order = part
    bufs = list(bufs)
    send_sem, recv_sem = bufs[-2:]
    own, paired = bufs[:2]
    pos = 2
    n = [0]

    def copy(src, dst, device):
        k = n[0]
        n[0] += 1
        cp = pltpu.make_async_remote_copy(
            src_ref=src,
            dst_ref=dst,
            send_sem=send_sem.at[k],
            recv_sem=recv_sem.at[k],
            device_id=device,
            device_id_type=MESH,
        )
        cp.start()
        sent.append(cp)
        return cp

    other = along(me, "c", 1)
    cp = copy(own.at[other], paired, moved(me, "c", 1))
    yield
    cp.wait_recv()

    @pl.loop(0, 16)
    def _(i):
        yi = lax.div(i, 4)
        zi = lax.rem(i, 4)
        total = own[me["c"], yi, zi].astype(F32) + paired[yi, zi].astype(F32)
        paired[yi, zi] = total.astype(BF16)

    data = paired
    dims = list(DIMS)
    for axis in order:
        r1r, r1l, r2r, r2l = bufs[pos : pos + 4]
        pos += 4
        at = dims.index(axis)
        rest = [d for d in dims if d != axis]

        def chunk(step):
            idx = [slice(None)] * len(dims)
            idx[at] = along(me, axis, step)
            return tuple(idx)

        def half(step, h):
            idx = [slice(None)] * (len(dims) + 1)
            idx[at] = along(me, axis, step)
            if rest:
                idx[dims.index(rest[0])] = pl.ds(2 * h, 2)
            else:
                idx[len(dims)] = pl.ds(16 * h, 16)
            return tuple(idx)

        right = moved(me, axis, 1)
        left = moved(me, axis, 3)
        cr = copy(data.at[half(2, 0)], r1r, right)
        cl = copy(data.at[half(2, 1)], r1l, left)
        yield
        cr.wait_recv()
        cl.wait_recv()
        i1 = half(1, 0)
        i3 = half(3, 1)
        data[i1] = (data[i1].astype(F32) + r1r[...].astype(F32)).astype(BF16)
        data[i3] = (data[i3].astype(F32) + r1l[...].astype(F32)).astype(BF16)
        cr = copy(data.at[chunk(1)], r2r, right)
        cl = copy(data.at[chunk(3)], r2l, left)
        yield
        cr.wait_recv()
        cl.wait_recv()
        total = data[chunk(0)].astype(F32) + r2r[...].astype(F32) + r2l[...].astype(F32)
        if rest:
            nxt = bufs[pos]
            pos += 1
            nxt[...] = total.astype(BF16)
            data = nxt
        else:
            w_out[:, c0 : c0 + width] = total
        dims = rest


def reduce_gain(me, slots, send_sem, recv_sem, sent):
    k = 0
    for stage, (axis, size) in enumerate((("c", 2), ("x", 4), ("y", 4), ("z", 4)), 1):
        cps = []
        slots[stage] = slots[0]
        first = k
        for step in range(1, size):
            cp = pltpu.make_async_remote_copy(
                src_ref=slots.at[stage],
                dst_ref=slots.at[5 + k],
                send_sem=send_sem.at[k],
                recv_sem=recv_sem.at[k],
                device_id=moved(me, axis, step),
                device_id_type=MESH,
            )
            cp.start()
            sent.append(cp)
            cps.append(cp)
            k += 1
        yield
        total = slots[stage]
        for i, cp in enumerate(cps):
            cp.wait_recv()
            total = total + slots[5 + first + i]
        slots[0] = total


def shift_up_rows(rows):
    moved_rows = pltpu.roll(rows, SEQ - (BLOCK - 1), 0)
    row = lax.broadcasted_iota(jnp.int32, rows.shape, 0)
    return jnp.where(row < SEQ - BLOCK + 1, moved_rows, 0.0)


def shift_down_rows(rows):
    moved_rows = pltpu.roll(rows, BLOCK - 1, 0)
    row = lax.broadcasted_iota(jnp.int32, rows.shape, 0)
    return jnp.where(row >= BLOCK - 1, moved_rows, 0.0)


def attention_block(b, q_ref, dm_ref, k_ref, v_ref, mixed_ref, dsh_ref):
    hr = lax.broadcasted_iota(jnp.int32, (256, 256), 0) // HD
    hc = lax.broadcasted_iota(jnp.int32, (256, 256), 1) // HD
    same = hr == hc
    hcol = lax.broadcasted_iota(jnp.int32, (64, 256), 1) // HD
    qrows = pl.ds(pl.multiple_of(b * 64, 64), 64)
    krows = pl.ds(pl.multiple_of(b * 256, 256), 256)

    def spread(rows):
        return jnp.where(same, jnp.concatenate([rows] * 4, axis=0), jnp.zeros((), BF16))

    def diag(full):
        out = full[0:64]
        for h in range(1, 4):
            out = jnp.where(hcol == h, full[h * 64 : h * 64 + 64], out)
        return out

    for g in range(4):
        cols = slice(g * 256, g * 256 + 256)
        qbd = spread(q_ref[qrows, cols])
        dobd = spread(dm_ref[qrows, cols])
        keys = k_ref[krows, cols]
        vals = v_ref[krows, cols]
        s = dot(keys, qbd, ((1,), (1,))) * HD ** (-0.5)
        e = jnp.exp(s - jnp.max(s, axis=0, keepdims=True))
        p = e * (1.0 / jnp.sum(e, axis=0, keepdims=True))
        pb = p.astype(BF16)
        mixed_ref[qrows, cols] = diag(dot(pb, vals, ((0,), (0,))))
        dp = dot(vals, dobd, ((1,), (1,)))
        v_ref[krows, cols] = dot(pb, dobd).astype(BF16)
        pdp = p * dp
        rd = jnp.sum(pdp, axis=0, keepdims=True)
        ds = ((pdp - p * rd) * HD ** (-0.5)).astype(BF16)
        dsh_ref[qrows, cols] = diag(dot(ds, keys, ((0,), (0,))))
        k_ref[krows, cols] = dot(ds, qbd).astype(BF16)


def step_kernel(
    x_ref, g_ref, gain_ref, w_ref, t_ref,
    out_ref, grad_ref, wsum_ref, gsum_ref,
    inv_ref, normed_ref, q_ref, dm_ref, k_ref, v_ref, mixed_ref, dsh_ref, dq_ref, attn_ref,
    tt_ref, at_ref, gslots, gsend, grecv, *part_bufs,
):
    me = my_coords()
    barrier = pltpu.get_barrier_semaphore()
    peers = [("c", 1)] + [(a, s) for a in ("x", "y", "z") for s in (1, 2, 3)]
    for axis, step in peers:
        pl.semaphore_signal(barrier, inc=1, device_id=moved(me, axis, step), device_id_type=MESH)
    pl.semaphore_wait(barrier, len(peers))

    @pl.loop(0, 2)
    def _(s):
        rows = pl.ds(pl.multiple_of(s * SEQ, SEQ), SEQ)
        x = x_ref[rows].astype(F32)
        inv = lax.rsqrt(jnp.mean(x * x, axis=1, keepdims=True) + EPSILON)
        inv_ref[rows] = inv
        normed = (x * inv * gain_ref[...]).astype(BF16)
        normed_ref[rows] = normed
        q_ref[rows] = shift_up_rows(dot(normed, w_ref[0])).astype(BF16)
        dm_ref[rows] = shift_up_rows(dot(g_ref[rows], w_ref[3], ((1,), (1,)))).astype(BF16)

    @pl.loop(0, 4)
    def _(i):
        rows = pl.ds(pl.multiple_of(i * 512, 512), 512)
        k_ref[rows] = dot(t_ref[rows], w_ref[1]).astype(BF16)
        v_ref[rows] = dot(t_ref[rows], w_ref[2]).astype(BF16)

    @pl.loop(0, 8)
    def _(b):
        attention_block(b, q_ref, dm_ref, k_ref, v_ref, mixed_ref, dsh_ref)

    @pl.loop(0, 8)
    def _(i):
        rows = pl.ds(pl.multiple_of(i * 256, 256), 256)
        tt_ref[:, rows] = t_ref[rows].T

    gslots[0] = jnp.zeros_like(gslots[0])

    @pl.loop(0, 2)
    def _(s):
        rows = pl.ds(pl.multiple_of(s * SEQ, SEQ), SEQ)
        x = x_ref[rows].astype(F32)
        inv = inv_ref[rows]
        attn = shift_down_rows(mixed_ref[rows]).astype(BF16)
        attn_ref[rows] = attn
        out_ref[rows] = (x + dot(attn, w_ref[3])).astype(BF16)
        dq = shift_down_rows(dsh_ref[rows]).astype(BF16)
        dq_ref[rows] = dq
        dn = dot(dq, w_ref[0], ((1,), (1,)))
        dnx = dn * x * inv
        gslots[0] += jnp.sum(dnx, axis=0, keepdims=True)
        dh = dn * gain_ref[...]
        inner = jnp.mean(dh * x, axis=1, keepdims=True)
        dx = inv * dh - x * (inv * inv * inv) * inner
        grad_ref[rows] = (g_ref[rows].astype(F32) + dx).astype(BF16)
        at_ref[0, :, rows] = normed_ref[rows].T
        at_ref[1, :, rows] = attn.T

    sent = []
    n_each = len(part_bufs) // 3
    flows = [reduce_gain(me, gslots, gsend, grecv, sent)]
    next(flows[0])
    for p, part in enumerate(PARTS):
        c0, width, _ = part
        bufs = part_bufs[p * n_each : (p + 1) * n_each]
        own = bufs[0]
        cols = slice(c0, c0 + width)

        @pl.loop(0, 4)
        def _(z):
            rows = pl.ds(pl.multiple_of(z * 256, 256), 256)
            for j in range(4):
                if j == 0:
                    res = dot(at_ref[0, rows, :], dq_ref[:, cols])
                elif j == 1:
                    res = dot(tt_ref[rows, :], k_ref[:, cols])
                elif j == 2:
                    res = dot(tt_ref[rows, :], v_ref[:, cols])
                else:
                    res = dot(at_ref[1, rows, :], g_ref[:, cols])
                res = res.astype(BF16)
                for xi in range(4):
                    for ci in range(2):
                        r0 = (xi * 2 + ci) * 32
                        own[ci, j, z, xi] = res[r0 : r0 + 32]

        flows.append(reduce_part(me, part, bufs, wsum_ref, sent))
        flows = [f for f in flows if next(f, True) is None]
    while flows:
        flows = [f for f in flows if next(f, True) is None]
    for cp in sent:
        cp.wait_send()
    gsum_ref[...] = gslots[0]


def train_step(hidden, cot, gains, weights, tiles):
    scratch = [
        pltpu.VMEM((512, 1), F32),
        pltpu.VMEM((512, D), BF16),
        pltpu.VMEM((512, D), BF16),
        pltpu.VMEM((512, D), BF16),
        pltpu.VMEM((2048, D), BF16),
        pltpu.VMEM((2048, D), BF16),
        pltpu.VMEM((512, D), F32),
        pltpu.VMEM((512, D), F32),
        pltpu.VMEM((512, D), BF16),
        pltpu.VMEM((512, D), BF16),
        pltpu.VMEM((D, 2048), BF16),
        pltpu.VMEM((2, D, 512), BF16),
        pltpu.VMEM((15, 1, D), F32),
        pltpu.SemaphoreType.DMA((10,)),
        pltpu.SemaphoreType.DMA((10,)),
    ]
    for part in PARTS:
        scratch += part_scratch(part)
    vmem = pl.BlockSpec(memory_space=pltpu.VMEM)
    return pl.pallas_call(
        step_kernel,
        out_shape=(
            jax.ShapeDtypeStruct((512, D), BF16),
            jax.ShapeDtypeStruct((512, D), BF16),
            jax.ShapeDtypeStruct((32, D), F32),
            jax.ShapeDtypeStruct((1, D), F32),
        ),
        in_specs=[vmem] * 5,
        out_specs=(vmem,) * 4,
        scratch_shapes=scratch,
        compiler_params=pltpu.CompilerParams(
            collective_id=1, has_side_effects=True, vmem_limit_bytes=62 * 1024 * 1024
        ),
        name="train_step",
    )(hidden, cot, gains, weights, tiles)


def fetch_tiles(library, neighbours, tile_home):
    n_lib = lax.axis_size("lib")
    lib_dev = library.shape[0]
    home_table = tile_home[0]
    wanted = neighbours.reshape(-1)
    n_requests = wanted.shape[0]
    is_wanted = wanted[:, None] == jnp.arange(home_table.shape[0], dtype=jnp.int32)[None, :]
    stored = jnp.sum(jnp.where(is_wanted, home_table[None, :], 0), axis=1)
    owner_dev = stored // lib_dev
    slot_idx = stored % lib_dev
    req_order = jnp.arange(n_requests, dtype=jnp.int32)
    same_before = (owner_dev[:, None] == owner_dev[None, :]) & (
        req_order[None, :] < req_order[:, None]
    )
    owner_rank = jnp.sum(same_before.astype(jnp.int32), axis=1)
    slot_hit = (owner_dev[:, None, None] == jnp.arange(n_lib, dtype=jnp.int32)[None, :, None]) & (
        owner_rank[:, None, None] == jnp.arange(CAP, dtype=jnp.int32)[None, None, :]
    )
    requested = jnp.sum(jnp.where(slot_hit, slot_idx[:, None, None], 0), axis=0)
    asked_slots = lax.all_to_all(requested, "lib", split_axis=0, concat_axis=0, tiled=True)
    picked = jnp.take(library, asked_slots.reshape(-1), axis=0)
    picked = picked.reshape(asked_slots.shape + library.shape[1:])
    arrived = lax.all_to_all(picked, "lib", split_axis=0, concat_axis=0, tiled=True)
    slot_rows = arrived.reshape((-1,) + library.shape[1:])
    my_tiles = jnp.take(slot_rows, owner_dev * CAP + owner_rank, axis=0)
    return my_tiles.reshape(-1, library.shape[-1])


def body(hidden_in, cotangent, gains, weights, library, neighbours, tile_home):
    tiles = fetch_tiles(library, neighbours, tile_home)
    out, grad, w_share, g_sum = train_step(hidden_in, cotangent, gains, weights[0], tiles)
    index = lax.axis_index("dp") * 8 + lax.axis_index("lib")
    g_share = lax.dynamic_slice(g_sum.reshape(-1), (index * 8,), (8,))
    return (out, grad, w_share, g_share)


def solution(mesh):
    return jax.shard_map(
        body,
        mesh=mesh,
        in_specs=(
            P(("dp", "lib"), None),
            P(("dp", "lib"), None),
            P(),
            P(),
            P(("dp", "lib"), None, None),
            P(("dp", "lib"), None),
            P("dp", None),
        ),
        out_specs=(
            P(("dp", "lib"), None),
            P(("dp", "lib"), None),
            P(("dp", "lib"), None),
            P(("dp", "lib")),
        ),
        check_vma=False,
    )
```

```python
import functools

import jax
import jax.numpy as jnp
from jax import lax
from jax.experimental import pallas as pl
from jax.experimental.pallas import tpu as pltpu
from jax.sharding import PartitionSpec as P

HD = 64
BLOCK = 64
CAP = 4
SEQ = 256
D = 1024
EPSILON = 1e-06

F32 = jnp.float32
BF16 = jnp.bfloat16
MESH = pl.DeviceIdType.MESH

PARTS = (
    (0, 384, ("x", "y", "z")),
    (384, 384, ("y", "z", "x")),
    (768, 256, ("z", "x", "y")),
)
DIMS = ("y", "z", "x")


def dot(left, right, dims=((1,), (0,))):
    return lax.dot_general(left, right, (dims, ((), ())), preferred_element_type=F32)


def my_coords():
    dp = lax.axis_index("dp")
    lib = lax.axis_index("lib")
    return {
        "y": lax.div(dp, 4),
        "z": lax.rem(dp, 4),
        "x": lax.div(lib, 2),
        "c": lax.rem(lib, 2),
    }


def device_of(at):
    return (at["y"] * 4 + at["z"], at["x"] * 2 + at["c"])


def along(me, axis, step):
    size = 2 if axis == "c" else 4
    return lax.rem(me[axis] + step, size)


def moved(me, axis, step):
    return device_of({**me, axis: along(me, axis, step)})


def stage_shapes(dims, width):
    rest = (4,) * (len(dims) - 1)
    chunk = rest + (32, width)
    half = ((2,) + rest[1:] + (32, width)) if rest else (16, width)
    return [half, half, chunk, chunk]


def part_scratch(part):
    _, width, order = part
    shapes = [pltpu.VMEM((4, 4, 4, 32, width), BF16)]
    dims = list(DIMS)
    n_copies = 1
    for pos, axis in enumerate(order):
        shapes += [pltpu.VMEM(s, BF16) for s in stage_shapes(dims, width)]
        n_copies += 4
        dims.remove(axis)
        if dims:
            shapes.append(pltpu.VMEM((4,) * len(dims) + (32, width), BF16))
    shapes += [pltpu.SemaphoreType.DMA((n_copies,)), pltpu.SemaphoreType.DMA((n_copies,))]
    return shapes


def reduce_part(me, part, own, bufs, w_out, sent):
    c0, width, order = part
    bufs = list(bufs)
    send_sem, recv_sem = bufs[-2:]
    paired = bufs[0]
    pos = 1
    cols = slice(c0, c0 + width)
    n = [0]

    def copy(src, dst, device):
        k = n[0]
        n[0] += 1
        cp = pltpu.make_async_remote_copy(
            src_ref=src,
            dst_ref=dst,
            send_sem=send_sem.at[k],
            recv_sem=recv_sem.at[k],
            device_id=device,
            device_id_type=MESH,
        )
        cp.start()
        sent.append(cp)
        return cp

    other = along(me, "c", 1)
    cp = copy(own.at[other, :, :, :, :, cols], paired, moved(me, "c", 1))
    yield
    cp.wait_recv()

    @pl.loop(0, 16)
    def _(i):
        yi = lax.div(i, 4)
        zi = lax.rem(i, 4)
        total = own[me["c"], yi, zi, :, :, cols].astype(F32) + paired[yi, zi].astype(F32)
        paired[yi, zi] = total.astype(BF16)

    data = paired
    dims = list(DIMS)
    for axis in order:
        r1r, r1l, r2r, r2l = bufs[pos : pos + 4]
        pos += 4
        at = dims.index(axis)
        rest = [d for d in dims if d != axis]

        def chunk(step):
            idx = [slice(None)] * len(dims)
            idx[at] = along(me, axis, step)
            return tuple(idx)

        def half(step, h):
            idx = [slice(None)] * (len(dims) + 1)
            idx[at] = along(me, axis, step)
            if rest:
                idx[dims.index(rest[0])] = pl.ds(2 * h, 2)
            else:
                idx[len(dims)] = pl.ds(16 * h, 16)
            return tuple(idx)

        right = moved(me, axis, 1)
        left = moved(me, axis, 3)
        cr = copy(data.at[half(2, 0)], r1r, right)
        cl = copy(data.at[half(2, 1)], r1l, left)
        yield
        cr.wait_recv()
        cl.wait_recv()
        i1 = half(1, 0)
        i3 = half(3, 1)
        data[i1] = (data[i1].astype(F32) + r1r[...].astype(F32)).astype(BF16)
        data[i3] = (data[i3].astype(F32) + r1l[...].astype(F32)).astype(BF16)
        cr = copy(data.at[chunk(1)], r2r, right)
        cl = copy(data.at[chunk(3)], r2l, left)
        yield
        cr.wait_recv()
        cl.wait_recv()
        total = data[chunk(0)].astype(F32) + r2r[...].astype(F32) + r2l[...].astype(F32)
        if rest:
            nxt = bufs[pos]
            pos += 1
            nxt[...] = total.astype(BF16)
            data = nxt
        else:
            w_out[:, c0 : c0 + width] = total
        dims = rest


def reduce_gain(me, slots, send_sem, recv_sem, sent):
    k = 0
    for stage, (axis, size) in enumerate((("c", 2), ("x", 4), ("y", 4), ("z", 4)), 1):
        cps = []
        slots[stage] = slots[0]
        first = k
        for step in range(1, size):
            cp = pltpu.make_async_remote_copy(
                src_ref=slots.at[stage],
                dst_ref=slots.at[5 + k],
                send_sem=send_sem.at[k],
                recv_sem=recv_sem.at[k],
                device_id=moved(me, axis, step),
                device_id_type=MESH,
            )
            cp.start()
            sent.append(cp)
            cps.append(cp)
            k += 1
        yield
        total = slots[stage]
        for i, cp in enumerate(cps):
            cp.wait_recv()
            total = total + slots[5 + first + i]
        slots[0] = total


def shift_up_rows(rows):
    moved_rows = pltpu.roll(rows, SEQ - (BLOCK - 1), 0)
    row = lax.broadcasted_iota(jnp.int32, rows.shape, 0)
    return jnp.where(row < SEQ - BLOCK + 1, moved_rows, 0.0)


def shift_down_rows(rows):
    moved_rows = pltpu.roll(rows, BLOCK - 1, 0)
    row = lax.broadcasted_iota(jnp.int32, rows.shape, 0)
    return jnp.where(row >= BLOCK - 1, moved_rows, 0.0)


def attention_block(b, q_ref, dm_ref, kv_ref, mixed_ref, dsh_ref):
    hr = lax.broadcasted_iota(jnp.int32, (256, 256), 0) // HD
    hc = lax.broadcasted_iota(jnp.int32, (256, 256), 1) // HD
    same = hr == hc
    hcol = lax.broadcasted_iota(jnp.int32, (64, 256), 1) // HD
    qrows = pl.ds(pl.multiple_of(b * 64, 64), 64)
    i = lax.div(b, 2)
    n = pl.ds(lax.rem(b, 2) * 2, 2)

    def spread(rows):
        return jnp.where(same, jnp.concatenate([rows] * 4, axis=0), jnp.zeros((), BF16))

    def diag(full):
        out = full[0:64]
        for h in range(1, 4):
            out = jnp.where(hcol == h, full[h * 64 : h * 64 + 64], out)
        return out

    for g in range(4):
        cols = slice(g * 256, g * 256 + 256)
        qbd = spread(q_ref[qrows, cols])
        dobd = spread(dm_ref[qrows, cols])
        keys = kv_ref[0, i, n, :, :, cols].reshape(256, 256)
        vals = kv_ref[1, i, n, :, :, cols].reshape(256, 256)
        s = dot(keys, qbd, ((1,), (1,))) * HD ** (-0.5)
        e = jnp.exp(s - jnp.max(s, axis=0, keepdims=True))
        p = e * (1.0 / jnp.sum(e, axis=0, keepdims=True))
        pb = p.astype(BF16)
        mixed_ref[qrows, cols] = diag(dot(pb, vals, ((0,), (0,)))).astype(BF16)
        dp = dot(vals, dobd, ((1,), (1,)))
        kv_ref[1, i, n, :, :, cols] = dot(pb, dobd).astype(BF16).reshape(2, 4, 32, 256)
        pdp = p * dp
        rd = jnp.sum(pdp, axis=0, keepdims=True)
        ds = ((pdp - p * rd) * HD ** (-0.5)).astype(BF16)
        dsh_ref[qrows, cols] = diag(dot(ds, keys, ((0,), (0,)))).astype(BF16)
        kv_ref[0, i, n, :, :, cols] = dot(ds, qbd).astype(BF16).reshape(2, 4, 32, 256)


LIB_PEERS = ((2, 0), (2, 1), (1, 0), (3, 0), (1, 1), (3, 1), (0, 1))


def lib_peer(me, dx, dc):
    return {**me, "x": along(me, "x", dx), "c": along(me, "c", dc)}


def start_fetch(me, req_ref, lib_ref, asked, asked_s, stage, slots, table_sems, tile_sems):
    mine = me["x"] * 2 + me["c"]
    tables = []
    for n, (dx, dc) in enumerate(LIB_PEERS):
        cp = pltpu.make_async_remote_copy(
            src_ref=req_ref,
            dst_ref=asked.at[mine],
            send_sem=table_sems.at[0, n],
            recv_sem=table_sems.at[1, n],
            device_id=device_of(lib_peer(me, dx, dc)),
            device_id_type=MESH,
        )
        cp.start()
        tables.append(cp)
    asked[mine] = req_ref[...]
    for cp in tables:
        cp.wait_recv()
    local = pltpu.make_async_copy(asked, asked_s, table_sems.at[0, 7])
    local.start()
    local.wait()
    tiles = []
    for n, (dx, dc) in enumerate(LIB_PEERS):
        at = lib_peer(me, dx, dc)
        peer = at["x"] * 2 + at["c"]
        box = stage.at[n // 4, n % 4]
        for k in range(CAP):
            box[k] = lib_ref[asked_s[peer, mine, k]]
        cp = pltpu.make_async_remote_copy(
            src_ref=box,
            dst_ref=slots.at[lax.div(mine, 4), lax.rem(mine, 4)],
            send_sem=tile_sems.at[0, n],
            recv_sem=tile_sems.at[1, n],
            device_id=device_of(at),
            device_id_type=MESH,
        )
        cp.start()
        tiles.append(cp)
    for k in range(CAP):
        slots[lax.div(mine, 4), lax.rem(mine, 4), k] = lib_ref[asked_s[mine, mine, k]]
    return tables, tiles


def step_kernel(
    x_ref, g_ref, gain_ref, w_ref, lib_ref, req_ref, order_ref,
    out_ref, grad_ref, wsum_ref, gsum_ref,
    inv_ref, q_ref, dm_ref, mixed_ref, dsh_ref, dq_ref, t_ref, tt_ref, at_ref, stage, slots,
    asked, asked_s, table_sems, tile_sems, gslots, gsend, grecv, *part_bufs,
):
    me = my_coords()
    barrier = pltpu.get_barrier_semaphore()
    peers = [lib_peer(me, dx, dc) for dx, dc in LIB_PEERS]
    peers += [{**me, a: along(me, a, s)} for a in ("y", "z") for s in (1, 2, 3)]
    for at in peers:
        pl.semaphore_signal(barrier, inc=1, device_id=device_of(at), device_id_type=MESH)
    pl.semaphore_wait(barrier, len(peers))

    tables, tiles = start_fetch(
        me, req_ref, lib_ref, asked, asked_s, stage, slots, table_sems, tile_sems
    )

    @pl.loop(0, 2)
    def _(s):
        rows = pl.ds(pl.multiple_of(s * SEQ, SEQ), SEQ)
        x = x_ref[rows].astype(F32)
        inv = lax.rsqrt(jnp.mean(x * x, axis=1, keepdims=True) + EPSILON)
        inv_ref[rows] = inv
        normed = (x * inv * gain_ref[...]).astype(BF16)
        at_ref[0, :, rows] = normed.T
        q_ref[rows] = shift_up_rows(dot(normed, w_ref[0])).astype(BF16)
        dm_ref[rows] = shift_up_rows(dot(g_ref[rows], w_ref[3], ((1,), (1,)))).astype(BF16)

    for cp in tiles:
        cp.wait_recv()

    @pl.loop(0, 16)
    def _(i):
        o = order_ref[i]
        t_ref[i] = slots[lax.div(o, 16), lax.rem(lax.div(o, 4), 4), lax.rem(o, 4)]

    @pl.loop(0, 4)
    def _(i):
        t = t_ref[pl.ds(i * 4, 4)].reshape(512, D)
        slots[0, i] = dot(t, w_ref[1]).astype(BF16).reshape(4, 4, 32, D)
        slots[1, i] = dot(t, w_ref[2]).astype(BF16).reshape(4, 4, 32, D)
        tt_ref[:, pl.ds(pl.multiple_of(i * 512, 512), 512)] = t.T

    @pl.loop(0, 8)
    def _(b):
        attention_block(b, q_ref, dm_ref, slots, mixed_ref, dsh_ref)

    gslots[0] = jnp.zeros_like(gslots[0])

    @pl.loop(0, 2)
    def _(s):
        rows = pl.ds(pl.multiple_of(s * SEQ, SEQ), SEQ)
        x = x_ref[rows].astype(F32)
        inv = inv_ref[rows]
        attn = shift_down_rows(mixed_ref[rows].astype(F32)).astype(BF16)
        at_ref[1, :, rows] = attn.T
        out_ref[rows] = (x + dot(attn, w_ref[3])).astype(BF16)
        dq = shift_down_rows(dsh_ref[rows].astype(F32)).astype(BF16)
        dq_ref[rows] = dq
        dn = dot(dq, w_ref[0], ((1,), (1,)))
        dnx = dn * x * inv
        gslots[0] += jnp.sum(dnx, axis=0, keepdims=True)
        dh = dn * gain_ref[...]
        inner = jnp.mean(dh * x, axis=1, keepdims=True)
        dx = inv * dh - x * (inv * inv * inv) * inner
        grad_ref[rows] = (g_ref[rows].astype(F32) + dx).astype(BF16)

    for cp in tiles:
        cp.wait_send()
    for cp in tables:
        cp.wait_send()
    sent = []
    n_each = len(part_bufs) // 3
    flows = [reduce_gain(me, gslots, gsend, grecv, sent)]
    next(flows[0])
    for p, part in enumerate(PARTS):
        c0, width, _ = part
        bufs = part_bufs[p * n_each : (p + 1) * n_each]
        cols = slice(c0, c0 + width)

        @pl.loop(0, 4)
        def _(z):
            rows = pl.ds(pl.multiple_of(z * 256, 256), 256)
            for j in range(4):
                if j == 0:
                    res = dot(at_ref[0, rows, :], dq_ref[:, cols])
                elif j == 3:
                    res = dot(at_ref[1, rows, :], g_ref[:, cols])
                else:
                    res = dot(tt_ref[rows, :], slots[j - 1, :, :, :, :, cols].reshape(2048, width))
                res = res.astype(BF16)
                for xi in range(4):
                    for ci in range(2):
                        r0 = (xi * 2 + ci) * 32
                        stage[ci, j, z, xi, :, cols] = res[r0 : r0 + 32]

        flows.append(reduce_part(me, part, stage, bufs, wsum_ref, sent))
        flows = [f for f in flows if next(f, True) is None]
    while flows:
        flows = [f for f in flows if next(f, True) is None]
    for cp in sent:
        cp.wait_send()
    gsum_ref[...] = gslots[0]


def train_step(hidden, cot, gains, weights, library, requested, order):
    rows5 = (2, 4, 4, 4, 32, D)
    scratch = [
        pltpu.VMEM((512, 1), F32),
        pltpu.VMEM((512, D), BF16),
        pltpu.VMEM((512, D), BF16),
        pltpu.VMEM((512, D), BF16),
        pltpu.VMEM((512, D), BF16),
        pltpu.VMEM((512, D), BF16),
        pltpu.VMEM((16, 4, 32, D), BF16),
        pltpu.VMEM((D, 2048), BF16),
        pltpu.VMEM((2, D, 512), BF16),
        pltpu.VMEM(rows5, BF16),
        pltpu.VMEM(rows5, BF16),
        pltpu.VMEM((8, 8, 128), jnp.int32),
        pltpu.SMEM((8, 8, 128), jnp.int32),
        pltpu.SemaphoreType.DMA((2, 8)),
        pltpu.SemaphoreType.DMA((2, 8)),
        pltpu.VMEM((15, 1, D), F32),
        pltpu.SemaphoreType.DMA((10,)),
        pltpu.SemaphoreType.DMA((10,)),
    ]
    for part in PARTS:
        scratch += part_scratch(part)
    vmem = pl.BlockSpec(memory_space=pltpu.VMEM)
    return pl.pallas_call(
        step_kernel,
        out_shape=(
            jax.ShapeDtypeStruct((512, D), BF16),
            jax.ShapeDtypeStruct((512, D), BF16),
            jax.ShapeDtypeStruct((32, D), F32),
            jax.ShapeDtypeStruct((1, D), F32),
        ),
        in_specs=[vmem] * 6 + [pl.BlockSpec(memory_space=pltpu.SMEM)],
        out_specs=(vmem,) * 4,
        scratch_shapes=scratch,
        compiler_params=pltpu.CompilerParams(
            collective_id=1, has_side_effects=True, vmem_limit_bytes=63 * 1024 * 1024
        ),
        name="train_step",
    )(hidden, cot, gains, weights, library.reshape(16, 4, 32, D), requested, order)


def requests(neighbours, tile_home):
    home_table = tile_home[0]
    wanted = neighbours.reshape(-1)
    is_wanted = wanted[:, None] == jnp.arange(128, dtype=jnp.int32)[None, :]
    stored = jnp.sum(jnp.where(is_wanted, home_table[None, :], 0), axis=1)
    owner = stored // 16
    slot = stored % 16
    i = jnp.arange(16, dtype=jnp.int32)
    same_before = (owner[:, None] == owner[None, :]) & (i[None, :] < i[:, None])
    rank = jnp.sum(same_before.astype(jnp.int32), axis=1)
    hit = (owner[:, None, None] == jnp.arange(8, dtype=jnp.int32)[None, :, None]) & (
        rank[:, None, None] == jnp.arange(128, dtype=jnp.int32)[None, None, :]
    )
    return jnp.sum(jnp.where(hit, slot[:, None, None], 0), axis=0), owner * CAP + rank


def body(hidden_in, cotangent, gains, weights, library, neighbours, tile_home):
    requested, order = requests(neighbours, tile_home)
    out, grad, w_share, g_sum = train_step(
        hidden_in, cotangent, gains, weights[0], library, requested, order
    )
    index = lax.axis_index("dp") * 8 + lax.axis_index("lib")
    g_share = lax.dynamic_slice(g_sum.reshape(-1), (index * 8,), (8,))
    return (out, grad, w_share, g_share)


def solution(mesh):
    return jax.shard_map(
        body,
        mesh=mesh,
        in_specs=(
            P(("dp", "lib"), None),
            P(("dp", "lib"), None),
            P(),
            P(),
            P(("dp", "lib"), None, None),
            P(("dp", "lib"), None),
            P("dp", None),
        ),
        out_specs=(
            P(("dp", "lib"), None),
            P(("dp", "lib"), None),
            P(("dp", "lib"), None),
            P(("dp", "lib")),
        ),
        check_vma=False,
    )
```

```python
import functools

import jax
import jax.numpy as jnp
from jax import lax
from jax.experimental import pallas as pl
from jax.experimental.pallas import tpu as pltpu
from jax.sharding import PartitionSpec as P

HD = 64
BLOCK = 64
CAP = 4
SEQ = 256
D = 1024
EPSILON = 1e-06

F32 = jnp.float32
BF16 = jnp.bfloat16
MESH = pl.DeviceIdType.MESH

ORDERS = (
    ("x", "y", "z"),
    ("y", "z", "x"),
    ("z", "x", "y"),
    ("x", "z", "y"),
    ("y", "x", "z"),
    ("z", "y", "x"),
    ("x", "y", "z"),
    ("z", "x", "y"),
)
PARTS = 4
DIMS = ("y", "z", "x")


def dot(left, right, dims=((1,), (0,))):
    return lax.dot_general(left, right, (dims, ((), ())), preferred_element_type=F32)


def my_coords():
    dp = lax.axis_index("dp")
    lib = lax.axis_index("lib")
    return {
        "y": lax.div(dp, 4),
        "z": lax.rem(dp, 4),
        "x": lax.div(lib, 2),
        "c": lax.rem(lib, 2),
    }


def device_of(at):
    return (at["y"] * 4 + at["z"], at["x"] * 2 + at["c"])


def along(me, axis, step):
    size = 2 if axis == "c" else 4
    return lax.rem(me[axis] + step, size)


def moved(me, axis, step):
    return device_of({**me, axis: along(me, axis, step)})


def piece_scratch():
    shapes = []
    for left in (2, 1, 0):
        block = (4,) * left + (32, 128)
        shapes.append(pltpu.VMEM((3,) + block, BF16))
        if left:
            shapes.append(pltpu.VMEM(block, BF16))
    shapes.append(pltpu.SemaphoreType.DMA((2, 9)))
    return shapes


def part_scratch():
    return [pltpu.VMEM((4, 4, 4, 32, 256), BF16), pltpu.SemaphoreType.DMA((2,))]


def start_pair(me, p, own, paired, sems):
    cols = slice(p * 256, p * 256 + 256)
    cp = pltpu.make_async_remote_copy(
        src_ref=own.at[along(me, "c", 1), :, :, :, :, cols],
        dst_ref=paired,
        send_sem=sems.at[0],
        recv_sem=sems.at[1],
        device_id=moved(me, "c", 1),
        device_id_type=MESH,
    )
    cp.start()
    return cp


def end_pair(me, p, own, paired, cp):
    cols = slice(p * 256, p * 256 + 256)
    cp.wait_recv()

    @pl.loop(0, 16)
    def _(i):
        yi = lax.div(i, 4)
        zi = lax.rem(i, 4)
        total = own[me["c"], yi, zi, :, :, cols].astype(F32) + paired[yi, zi].astype(F32)
        paired[yi, zi] = total.astype(BF16)


def reduce_piece(me, q, data, bufs, w_out, sent):
    sems = bufs[-1]
    dims = list(DIMS)
    n = 0
    for pos, axis in enumerate(ORDERS[q]):
        recv = bufs[2 * pos]
        at = dims.index(axis)

        def chunk(step):
            idx = [slice(None)] * len(dims)
            idx[at] = along(me, axis, step)
            return tuple(idx)

        cps = []
        for step in (2, 1, 3):
            cp = pltpu.make_async_remote_copy(
                src_ref=data.at[chunk(step)],
                dst_ref=recv.at[step - 1],
                send_sem=sems.at[0, n],
                recv_sem=sems.at[1, n],
                device_id=moved(me, axis, step),
                device_id_type=MESH,
            )
            cp.start()
            sent.append(cp)
            cps.append(cp)
            n += 1
        yield
        for cp in cps:
            cp.wait_recv()
        total = data[chunk(0)].astype(F32)
        for k in range(3):
            total = total + recv[k].astype(F32)
        if pos < 2:
            data = bufs[2 * pos + 1]
            data[...] = total.astype(BF16)
        else:
            w_out[:, q * 128 : q * 128 + 128] = total
        dims.remove(axis)


def reduce_gain(me, slots, send_sem, recv_sem, sent):
    k = 0
    for stage, axis in enumerate(("lib", "y", "z"), 1):
        if axis == "lib":
            peers = [lib_peer(me, dx, dc) for dx, dc in LIB_PEERS]
        else:
            peers = [{**me, axis: along(me, axis, step)} for step in (1, 2, 3)]
        slots[stage] = slots[0]
        cps = []
        first = k
        for at in peers:
            cp = pltpu.make_async_remote_copy(
                src_ref=slots.at[stage],
                dst_ref=slots.at[4 + k],
                send_sem=send_sem.at[k],
                recv_sem=recv_sem.at[k],
                device_id=device_of(at),
                device_id_type=MESH,
            )
            cp.start()
            sent.append(cp)
            cps.append(cp)
            k += 1
        yield
        total = slots[stage]
        for i, cp in enumerate(cps):
            cp.wait_recv()
            total = total + slots[4 + first + i]
        slots[0] = total


def shift_up_rows(rows):
    moved_rows = pltpu.roll(rows, SEQ - (BLOCK - 1), 0)
    row = lax.broadcasted_iota(jnp.int32, rows.shape, 0)
    return jnp.where(row < SEQ - BLOCK + 1, moved_rows, 0.0)


def shift_down_rows(rows):
    moved_rows = pltpu.roll(rows, BLOCK - 1, 0)
    row = lax.broadcasted_iota(jnp.int32, rows.shape, 0)
    return jnp.where(row >= BLOCK - 1, moved_rows, 0.0)


def attention_block(b, q_ref, dm_ref, kv_ref, mixed_ref, dsh_ref):
    hr = lax.broadcasted_iota(jnp.int32, (256, 256), 0) // HD
    hc = lax.broadcasted_iota(jnp.int32, (256, 256), 1) // HD
    same = hr == hc
    hcol = lax.broadcasted_iota(jnp.int32, (64, 256), 1) // HD
    qrows = pl.ds(pl.multiple_of(b * 64, 64), 64)
    i = lax.div(b, 2)
    n = pl.ds(lax.rem(b, 2) * 2, 2)

    def spread(rows):
        return jnp.where(same, jnp.concatenate([rows] * 4, axis=0), jnp.zeros((), BF16))

    def diag(full):
        out = full[0:64]
        for h in range(1, 4):
            out = jnp.where(hcol == h, full[h * 64 : h * 64 + 64], out)
        return out

    groups = [slice(g * 256, g * 256 + 256) for g in range(4)]
    qbd = [spread(q_ref[qrows, c]) for c in groups]
    dobd = [spread(dm_ref[qrows, c]) for c in groups]
    keys = [kv_ref[0, i, n, :, :, c].reshape(256, 256) for c in groups]
    vals = [kv_ref[1, i, n, :, :, c].reshape(256, 256) for c in groups]
    score = [dot(k, q, ((1,), (1,))) * HD ** (-0.5) for k, q in zip(keys, qbd)]
    dp = [dot(v, d, ((1,), (1,))) for v, d in zip(vals, dobd)]
    e = [jnp.exp(a - jnp.max(a, axis=0, keepdims=True)) for a in score]
    p = [a * (1.0 / jnp.sum(a, axis=0, keepdims=True)) for a in e]
    pb = [a.astype(BF16) for a in p]
    pdp = [a * d for a, d in zip(p, dp)]
    rd = [jnp.sum(a, axis=0, keepdims=True) for a in pdp]
    ds = [((a - w * r) * HD ** (-0.5)).astype(BF16) for a, w, r in zip(pdp, p, rd)]
    mixed = [diag(dot(a, v, ((0,), (0,)))).astype(BF16) for a, v in zip(pb, vals)]
    dv = [dot(a, d).astype(BF16).reshape(2, 4, 32, 256) for a, d in zip(pb, dobd)]
    dsh = [diag(dot(a, k, ((0,), (0,)))).astype(BF16) for a, k in zip(ds, keys)]
    dk = [dot(a, q).astype(BF16).reshape(2, 4, 32, 256) for a, q in zip(ds, qbd)]
    for g, c in enumerate(groups):
        mixed_ref[qrows, c] = mixed[g]
        dsh_ref[qrows, c] = dsh[g]
        kv_ref[1, i, n, :, :, c] = dv[g]
        kv_ref[0, i, n, :, :, c] = dk[g]


LIB_PEERS = ((2, 0), (2, 1), (1, 0), (3, 0), (1, 1), (3, 1), (0, 1))


def lib_peer(me, dx, dc):
    return {**me, "x": along(me, "x", dx), "c": along(me, "c", dc)}


def start_fetch(me, req_ref, lib_ref, lib_load, asked, asked_s, stage, slots, table_sems, tile_sems):
    mine = me["x"] * 2 + me["c"]
    tables = []
    for n, (dx, dc) in enumerate(LIB_PEERS):
        cp = pltpu.make_async_remote_copy(
            src_ref=req_ref,
            dst_ref=asked.at[mine],
            send_sem=table_sems.at[0, n],
            recv_sem=table_sems.at[1, n],
            device_id=device_of(lib_peer(me, dx, dc)),
            device_id_type=MESH,
        )
        cp.start()
        tables.append(cp)
    asked[mine] = req_ref[...]
    for cp in tables:
        cp.wait_recv()
    local = pltpu.make_async_copy(asked, asked_s, table_sems.at[0, 7])
    local.start()
    local.wait()
    lib_load.wait()
    tiles = []
    for n, (dx, dc) in enumerate(LIB_PEERS):
        at = lib_peer(me, dx, dc)
        peer = at["x"] * 2 + at["c"]
        box = stage.at[n // 4, n % 4]
        for k in range(CAP):
            box[k] = lib_ref[asked_s[peer, mine, k]]
        cp = pltpu.make_async_remote_copy(
            src_ref=box,
            dst_ref=slots.at[lax.div(mine, 4), lax.rem(mine, 4)],
            send_sem=tile_sems.at[0, n],
            recv_sem=tile_sems.at[1, n],
            device_id=device_of(at),
            device_id_type=MESH,
        )
        cp.start()
        tiles.append(cp)
    for k in range(CAP):
        slots[lax.div(mine, 4), lax.rem(mine, 4), k] = lib_ref[asked_s[mine, mine, k]]
    return tables, tiles


def step_kernel(
    x_hbm, g_hbm, gain_ref, w_hbm, lib_hbm, req_ref, order_ref,
    out_ref, grad_ref, wsum_ref, gsum_ref,
    x_ref, g_ref, w_ref, lib_ref, load_sems,
    inv_ref, q_ref, dm_ref, mixed_ref, dsh_ref, t_ref, tt_ref, at_ref, stage, slots,
    asked, asked_s, table_sems, tile_sems, gslots, gsend, grecv, *sum_bufs,
):
    me = my_coords()
    loads = []
    pairs = [(lib_hbm, lib_ref), (x_hbm, x_ref), (w_hbm.at[0], w_ref.at[0]), (g_hbm, g_ref)]
    pairs += [(w_hbm.at[j], w_ref.at[j]) for j in (3, 1, 2)]
    for n, (src, dst) in enumerate(pairs):
        cp = pltpu.make_async_copy(src, dst, load_sems.at[n])
        cp.start()
        loads.append(cp)

    barrier = pltpu.get_barrier_semaphore()
    peers = [lib_peer(me, dx, dc) for dx, dc in LIB_PEERS]
    peers += [{**me, a: along(me, a, s)} for a in ("y", "z") for s in (1, 2, 3)]
    for at in peers:
        pl.semaphore_signal(barrier, inc=1, device_id=device_of(at), device_id_type=MESH)
    pl.semaphore_wait(barrier, len(peers))

    tables, tiles = start_fetch(
        me, req_ref, lib_ref, loads[0], asked, asked_s, stage, slots, table_sems, tile_sems
    )

    for cp in loads[1:5]:
        cp.wait()

    @pl.loop(0, 2)
    def _(s):
        rows = pl.ds(pl.multiple_of(s * SEQ, SEQ), SEQ)
        x = x_ref[rows].astype(F32)
        inv = lax.rsqrt(jnp.mean(x * x, axis=1, keepdims=True) + EPSILON)
        inv_ref[rows] = inv
        normed = (x * inv * gain_ref[...]).astype(BF16)
        at_ref[0, :, rows] = normed.T
        q_ref[rows] = shift_up_rows(dot(normed, w_ref[0])).astype(BF16)
        dm_ref[rows] = shift_up_rows(dot(g_ref[rows], w_ref[3], ((1,), (1,)))).astype(BF16)

    for cp in loads[5:]:
        cp.wait()
    for cp in tiles:
        cp.wait_recv()

    @pl.loop(0, 16)
    def _(i):
        o = order_ref[i]
        t_ref[i] = slots[lax.div(o, 16), lax.rem(lax.div(o, 4), 4), lax.rem(o, 4)]

    @pl.loop(0, 4)
    def _(i):
        t = t_ref[pl.ds(i * 4, 4)].reshape(512, D)
        slots[0, i] = dot(t, w_ref[1]).astype(BF16).reshape(4, 4, 32, D)
        slots[1, i] = dot(t, w_ref[2]).astype(BF16).reshape(4, 4, 32, D)
        tt_ref[:, pl.ds(pl.multiple_of(i * 512, 512), 512)] = t.T

    @pl.loop(0, 8)
    def _(b):
        attention_block(b, q_ref, dm_ref, slots, mixed_ref, dsh_ref)

    @pl.loop(0, 2)
    def _(s):
        rows = pl.ds(pl.multiple_of(s * SEQ, SEQ), SEQ)
        attn = shift_down_rows(mixed_ref[rows].astype(F32)).astype(BF16)
        mixed_ref[rows] = attn
        at_ref[1, :, rows] = attn.T
        dsh_ref[rows] = shift_down_rows(dsh_ref[rows].astype(F32)).astype(BF16)

    for cp in tiles:
        cp.wait_send()
    for cp in tables:
        cp.wait_send()

    def weight_terms(p):
        cols = slice(p * 256, p * 256 + 256)

        @pl.loop(0, 4)
        def _(z):
            rows = pl.ds(pl.multiple_of(z * 256, 256), 256)
            for j in range(4):
                if j == 0:
                    res = dot(at_ref[0, rows, :], dsh_ref[:, cols])
                elif j == 3:
                    res = dot(at_ref[1, rows, :], g_ref[:, cols])
                else:
                    res = dot(tt_ref[rows, :], slots[j - 1, :, :, :, :, cols].reshape(2048, 256))
                res = res.astype(BF16)
                for xi in range(4):
                    for ci in range(2):
                        r0 = (xi * 2 + ci) * 32
                        stage[ci, j, z, xi, :, cols] = res[r0 : r0 + 32]

    def row_results(s):
        rows = pl.ds(s * SEQ, SEQ)
        x = x_ref[rows].astype(F32)
        inv = inv_ref[rows]
        out_ref[rows] = (x + dot(mixed_ref[rows], w_ref[3])).astype(BF16)
        dn = dot(dsh_ref[rows], w_ref[0], ((1,), (1,)))
        dnx = dn * x * inv
        term = jnp.sum(dnx, axis=0, keepdims=True)
        gslots[0] = term if s == 0 else gslots[0] + term
        dh = dn * gain_ref[...]
        inner = jnp.mean(dh * x, axis=1, keepdims=True)
        dx = inv * dh - x * (inv * inv * inv) * inner
        grad_ref[rows] = (g_ref[rows].astype(F32) + dx).astype(BF16)

    sent = []
    part_bufs = sum_bufs[: 2 * PARTS]
    piece_bufs = sum_bufs[2 * PARTS :]
    n_each = len(piece_bufs) // (2 * PARTS)
    pair = {}
    flow = {}

    def send_part(p):
        pair[p] = start_pair(me, p, stage, *part_bufs[2 * p : 2 * p + 2])
        sent.append(pair[p])

    def sum_part(p):
        paired = part_bufs[2 * p]
        end_pair(me, p, stage, paired, pair[p])
        flow[p] = []
        for h in range(2):
            q = 2 * p + h
            bufs = piece_bufs[q * n_each : (q + 1) * n_each]
            data = paired.at[:, :, :, :, pl.ds(h * 128, 128)]
            flow[p].append(reduce_piece(me, q, data, bufs, wsum_ref, sent))
            next(flow[p][-1])

    def advance(p):
        for f in flow[p]:
            next(f, None)

    weight_terms(0)
    send_part(0)
    weight_terms(1)
    send_part(1)
    sum_part(0)
    weight_terms(2)
    send_part(2)
    sum_part(1)
    weight_terms(3)
    send_part(3)
    sum_part(2)
    advance(0)
    row_results(0)
    sum_part(3)
    advance(1)
    advance(0)
    row_results(1)
    gain_flow = reduce_gain(me, gslots, gsend, grecv, sent)
    next(gain_flow)
    advance(2)
    advance(1)
    advance(0)
    next(gain_flow)
    advance(3)
    advance(2)
    advance(1)
    next(gain_flow)
    advance(3)
    advance(2)
    next(gain_flow, None)
    advance(3)
    for cp in sent:
        cp.wait_send()
    index = lax.axis_index("dp") * 8 + lax.axis_index("lib")
    gsum_ref[...] = pltpu.roll(gslots[0], lax.rem(D - index * 8, D), 1)[:, :128]


def train_step(hidden, cot, gains, weights, library, requested, order):
    rows5 = (2, 4, 4, 4, 32, D)
    scratch = [
        pltpu.VMEM((512, D), BF16),
        pltpu.VMEM((512, D), BF16),
        pltpu.VMEM((4, D, D), BF16),
        pltpu.VMEM((16, 4, 32, D), BF16),
        pltpu.SemaphoreType.DMA((7,)),
        pltpu.VMEM((512, 1), F32),
        pltpu.VMEM((512, D), BF16),
        pltpu.VMEM((512, D), BF16),
        pltpu.VMEM((512, D), BF16),
        pltpu.VMEM((512, D), BF16),
        pltpu.VMEM((16, 4, 32, D), BF16),
        pltpu.VMEM((D, 2048), BF16),
        pltpu.VMEM((2, D, 512), BF16),
        pltpu.VMEM(rows5, BF16),
        pltpu.VMEM(rows5, BF16),
        pltpu.VMEM((8, 8, 128), jnp.int32),
        pltpu.SMEM((8, 8, 128), jnp.int32),
        pltpu.SemaphoreType.DMA((2, 8)),
        pltpu.SemaphoreType.DMA((2, 8)),
        pltpu.VMEM((17, 1, D), F32),
        pltpu.SemaphoreType.DMA((13,)),
        pltpu.SemaphoreType.DMA((13,)),
    ]
    for _ in range(PARTS):
        scratch += part_scratch()
    for _ in range(2 * PARTS):
        scratch += piece_scratch()
    hbm = pl.BlockSpec(memory_space=pl.ANY)
    vmem = pl.BlockSpec(memory_space=pltpu.VMEM)
    return pl.pallas_call(
        step_kernel,
        out_shape=(
            jax.ShapeDtypeStruct((512, D), BF16),
            jax.ShapeDtypeStruct((512, D), BF16),
            jax.ShapeDtypeStruct((32, D), F32),
            jax.ShapeDtypeStruct((1, 128), F32),
        ),
        in_specs=[hbm, hbm, vmem, hbm, hbm, vmem, pl.BlockSpec(memory_space=pltpu.SMEM)],
        out_specs=(vmem,) * 4,
        scratch_shapes=scratch,
        compiler_params=pltpu.CompilerParams(
            collective_id=1, has_side_effects=True, vmem_limit_bytes=63 * 1024 * 1024
        ),
        name="train_step",
    )(hidden, cot, gains, weights, library.reshape(16, 4, 32, D), requested, order)


def requests(neighbours, tile_home):
    home_table = tile_home[0]
    wanted = neighbours.reshape(-1)
    is_wanted = wanted[:, None] == jnp.arange(128, dtype=jnp.int32)[None, :]
    stored = jnp.sum(jnp.where(is_wanted, home_table[None, :], 0), axis=1)
    owner = stored // 16
    slot = stored % 16
    i = jnp.arange(16, dtype=jnp.int32)
    same_before = (owner[:, None] == owner[None, :]) & (i[None, :] < i[:, None])
    rank = jnp.sum(same_before.astype(jnp.int32), axis=1)
    hit = (owner[:, None, None] == jnp.arange(8, dtype=jnp.int32)[None, :, None]) & (
        rank[:, None, None] == jnp.arange(128, dtype=jnp.int32)[None, None, :]
    )
    return jnp.sum(jnp.where(hit, slot[:, None, None], 0), axis=0), owner * CAP + rank


def body(hidden_in, cotangent, gains, weights, library, neighbours, tile_home):
    requested, order = requests(neighbours, tile_home)
    out, grad, w_share, g_sum = train_step(
        hidden_in, cotangent, gains, weights[0], library, requested, order
    )
    g_share = g_sum[0, :8]
    return (out, grad, w_share, g_share)


def solution(mesh):
    return jax.shard_map(
        body,
        mesh=mesh,
        in_specs=(
            P(("dp", "lib"), None),
            P(("dp", "lib"), None),
            P(),
            P(),
            P(("dp", "lib"), None, None),
            P(("dp", "lib"), None),
            P("dp", None),
        ),
        out_specs=(
            P(("dp", "lib"), None),
            P(("dp", "lib"), None),
            P(("dp", "lib"), None),
            P(("dp", "lib")),
        ),
        check_vma=False,
    )
```

```python
import functools

import jax
import jax.numpy as jnp
from jax import lax
from jax.experimental import pallas as pl
from jax.experimental.pallas import tpu as pltpu
from jax.sharding import PartitionSpec as P

HD = 64
BLOCK = 64
CAP = 4
SEQ = 256
D = 1024
EPSILON = 1e-06

F32 = jnp.float32
BF16 = jnp.bfloat16
MESH = pl.DeviceIdType.MESH

ORDERS = (
    ("x", "y", "z"),
    ("y", "z", "x"),
    ("z", "x", "y"),
    ("x", "z", "y"),
    ("y", "x", "z"),
    ("z", "y", "x"),
    ("x", "y", "z"),
    ("z", "x", "y"),
)
PARTS = 4
DIMS = ("y", "z", "x")


def dot(left, right, dims=((1,), (0,))):
    return lax.dot_general(left, right, (dims, ((), ())), preferred_element_type=F32)


def my_coords():
    dp = lax.axis_index("dp")
    lib = lax.axis_index("lib")
    return {
        "y": lax.div(dp, 4),
        "z": lax.rem(dp, 4),
        "x": lax.div(lib, 2),
        "c": lax.rem(lib, 2),
    }


def device_of(at):
    return (at["y"] * 4 + at["z"], at["x"] * 2 + at["c"])


def along(me, axis, step):
    size = 2 if axis == "c" else 4
    return lax.rem(me[axis] + step, size)


def moved(me, axis, step):
    return device_of({**me, axis: along(me, axis, step)})


def piece_scratch():
    shapes = []
    for left in (2, 1, 0):
        block = (4,) * left + (32, 128)
        shapes.append(pltpu.VMEM((3,) + block, BF16))
    shapes.append(pltpu.SemaphoreType.DMA((2, 9)))
    return shapes


def start_pair(me, p, own, paired, sems):
    cols = slice(p * 256, p * 256 + 256)
    cp = pltpu.make_async_remote_copy(
        src_ref=own.at[along(me, "c", 1), :, :, :, :, cols],
        dst_ref=paired.at[:, :, :, :, cols],
        send_sem=sems.at[0, p],
        recv_sem=sems.at[1, p],
        device_id=moved(me, "c", 1),
        device_id_type=MESH,
    )
    cp.start()
    return cp


def end_pair(me, p, own, paired, cp):
    cols = slice(p * 256, p * 256 + 256)
    cp.wait_recv()

    @pl.loop(0, 16)
    def _(i):
        yi = lax.div(i, 4)
        zi = lax.rem(i, 4)
        total = own[me["c"], yi, zi, :, :, cols].astype(F32)
        total = total + paired[yi, zi, :, :, cols].astype(F32)
        paired[yi, zi, :, :, cols] = total.astype(BF16)


def reduce_piece(me, q, data, bufs, w_out, sent):
    sems = bufs[-1]
    dims = list(DIMS)
    n = 0
    for pos, axis in enumerate(ORDERS[q]):
        recv = bufs[pos]
        at = dims.index(axis)

        def chunk(step):
            idx = [slice(None)] * len(dims)
            idx[at] = along(me, axis, step)
            return tuple(idx)

        cps = []
        for step in (2, 1, 3):
            cp = pltpu.make_async_remote_copy(
                src_ref=data.at[chunk(step)],
                dst_ref=recv.at[step - 1],
                send_sem=sems.at[0, n],
                recv_sem=sems.at[1, n],
                device_id=moved(me, axis, step),
                device_id_type=MESH,
            )
            cp.start()
            sent.append(cp)
            cps.append(cp)
            n += 1
        yield
        for cp in cps:
            cp.wait_recv()
        total = data[chunk(0)].astype(F32)
        for k in range(3):
            total = total + recv[k].astype(F32)
        if pos < 2:
            data = recv.at[0]
            data[...] = total.astype(BF16)
        else:
            w_out[:, q * 128 : q * 128 + 128] = total
        dims.remove(axis)


def reduce_gain(me, slots, send_sem, recv_sem, sent):
    k = 0
    for stage, axis in enumerate(("lib", "y", "z"), 1):
        if axis == "lib":
            peers = [lib_peer(me, dx, dc) for dx, dc in LIB_PEERS]
        else:
            peers = [{**me, axis: along(me, axis, step)} for step in (1, 2, 3)]
        slots[stage] = slots[0]
        cps = []
        first = k
        for at in peers:
            cp = pltpu.make_async_remote_copy(
                src_ref=slots.at[stage],
                dst_ref=slots.at[4 + k],
                send_sem=send_sem.at[k],
                recv_sem=recv_sem.at[k],
                device_id=device_of(at),
                device_id_type=MESH,
            )
            cp.start()
            sent.append(cp)
            cps.append(cp)
            k += 1
        yield
        total = slots[stage]
        for i, cp in enumerate(cps):
            cp.wait_recv()
            total = total + slots[4 + first + i]
        slots[0] = total


def shift_up_rows(rows):
    moved_rows = pltpu.roll(rows, SEQ - (BLOCK - 1), 0)
    row = lax.broadcasted_iota(jnp.int32, rows.shape, 0)
    return jnp.where(row < SEQ - BLOCK + 1, moved_rows, 0.0)


def shift_down_rows(rows):
    moved_rows = pltpu.roll(rows, BLOCK - 1, 0)
    row = lax.broadcasted_iota(jnp.int32, rows.shape, 0)
    return jnp.where(row >= BLOCK - 1, moved_rows, 0.0)


def head_of(shape, dim):
    return lax.broadcasted_iota(jnp.int32, shape, dim) // HD


def spread(rows):
    same = head_of((256, 256), 0) == head_of((256, 256), 1)
    return jnp.where(same, jnp.concatenate([rows] * 4, axis=0), jnp.zeros((), BF16))


def diag(full):
    hcol = head_of((64, 256), 1)
    out = full[0:64]
    for h in range(1, 4):
        out = jnp.where(hcol == h, full[h * 64 : h * 64 + 64], out)
    return out


def block_rows(b):
    return pl.ds(pl.multiple_of(b * 64, 64), 64)


def block_tiles(b):
    return lax.div(b, 2), pl.ds(lax.rem(b, 2) * 2, 2)


def slot_rows(ref, order_ref, b, c):
    tiles = [ref[order_ref[b * 2 + n], :, :, c].reshape(128, 256) for n in range(2)]
    return jnp.concatenate(tiles, axis=0)


def attend(b, order_ref, q_ref, k_ref, v_ref, prob_ref, mixed_ref):
    groups = [slice(g * 256, g * 256 + 256) for g in range(4)]
    rows = block_rows(b)
    qbd = [spread(q_ref[rows, c]) for c in groups]
    keys = [slot_rows(k_ref, order_ref, b, c) for c in groups]
    vals = [slot_rows(v_ref, order_ref, b, c) for c in groups]
    score = [dot(k, q, ((1,), (1,))) * HD ** (-0.5) for k, q in zip(keys, qbd)]
    e = [jnp.exp(a - jnp.max(a, axis=0, keepdims=True)) for a in score]
    pb = [(a * (1.0 / jnp.sum(a, axis=0, keepdims=True))).astype(BF16) for a in e]
    mixed = [diag(dot(a, v, ((0,), (0,)))).astype(BF16) for a, v in zip(pb, vals)]
    for g, c in enumerate(groups):
        prob_ref[pl.ds(b * 2, 2), :, :, c] = pb[g].reshape(2, 4, 32, 256)
        mixed_ref[rows, c] = mixed[g]


def attend_back(b0, n_blocks, g, order_ref, q_ref, dm_ref, k_ref, v_ref, prob_ref, dkv_ref, dsh_ref):
    c = slice(g * 256, g * 256 + 256)
    blocks = [b0 + k for k in range(n_blocks)]
    at = [block_tiles(b) for b in blocks]
    qbd = [spread(q_ref[block_rows(b), c]) for b in blocks]
    dobd = [spread(dm_ref[block_rows(b), c]) for b in blocks]
    keys = [slot_rows(k_ref, order_ref, b, c) for b in blocks]
    vals = [slot_rows(v_ref, order_ref, b, c) for b in blocks]
    pb = [prob_ref[pl.ds(b * 2, 2), :, :, c].reshape(256, 256) for b in blocks]
    dp = [dot(v, d, ((1,), (1,))) for v, d in zip(vals, dobd)]
    dv = [dot(a, d).astype(BF16).reshape(2, 4, 32, 256) for a, d in zip(pb, dobd)]
    p = [a.astype(F32) for a in pb]
    pdp = [a * d for a, d in zip(p, dp)]
    rd = [
        jnp.sum(w, axis=0, keepdims=True) * (1.0 / jnp.sum(a, axis=0, keepdims=True))
        for w, a in zip(pdp, p)
    ]
    ds = [((w - a * r) * HD ** (-0.5)).astype(BF16) for w, a, r in zip(pdp, p, rd)]
    dsh = [diag(dot(a, k, ((0,), (0,)))).astype(BF16) for a, k in zip(ds, keys)]
    dk = [dot(a, q).astype(BF16).reshape(2, 4, 32, 256) for a, q in zip(ds, qbd)]
    for k, b in enumerate(blocks):
        i, n = at[k]
        dsh_ref[block_rows(b), c] = dsh[k]
        dkv_ref[1, i, n, :, :, c] = dv[k]
        dkv_ref[0, i, n, :, :, c] = dk[k]


LIB_PEERS = ((2, 0), (2, 1), (1, 0), (3, 0), (1, 1), (3, 1), (0, 1))


def lib_peer(me, dx, dc):
    return {**me, "x": along(me, "x", dx), "c": along(me, "c", dc)}


def request_table(wanted, home, order):
    row = lax.broadcasted_iota(jnp.int32, (8, 128), 0)
    col = lax.broadcasted_iota(jnp.int32, (8, 128), 1)
    table = jnp.zeros((8, 128), jnp.int32)
    owners = []
    for i in range(16):
        stored = home[0, wanted[i // 2, i % 2]]
        owner = lax.div(stored, 16)
        rank = jnp.int32(0)
        for before in owners:
            rank = rank + jnp.where(before == owner, 1, 0)
        owners.append(owner)
        order[i] = owner * CAP + rank
        table = jnp.where((row == owner) & (col == rank), lax.rem(stored, 16), table)
    return table


def start_fetch(me, req_ref, lib_ref, loads, asked, asked_s, stage, slots, table_sems, tile_sems):
    mine = me["x"] * 2 + me["c"]
    tables = []
    for n, (dx, dc) in enumerate(LIB_PEERS):
        cp = pltpu.make_async_remote_copy(
            src_ref=req_ref,
            dst_ref=asked.at[mine],
            send_sem=table_sems.at[0, n],
            recv_sem=table_sems.at[1, n],
            device_id=device_of(lib_peer(me, dx, dc)),
            device_id_type=MESH,
        )
        cp.start()
        tables.append(cp)
    asked[mine] = req_ref[...]
    for cp in tables:
        cp.wait_recv()
    local = pltpu.make_async_copy(asked, asked_s, table_sems.at[0, 7])
    local.start()
    local.wait()
    loads[0].wait()
    own_box = (lax.div(mine, 4), lax.rem(mine, 4))
    waves = []
    for k in range(CAP):
        wave = []
        for n, (dx, dc) in enumerate(LIB_PEERS):
            cp = pltpu.make_async_remote_copy(
                src_ref=stage.at[n // 4, n % 4, k],
                dst_ref=slots.at[own_box[0], own_box[1], k],
                send_sem=tile_sems.at[0, n * CAP + k],
                recv_sem=tile_sems.at[1, n * CAP + k],
                device_id=device_of(lib_peer(me, dx, dc)),
                device_id_type=MESH,
            )
            wave.append(cp)
        waves.append(wave)

    def stage_tile(n, k):
        at = lib_peer(me, *LIB_PEERS[n])
        peer = at["x"] * 2 + at["c"]
        stage[n // 4, n % 4, k] = lib_ref[asked_s[peer, mine, k]]

    for n in range(len(LIB_PEERS)):
        stage_tile(n, 0)
        waves[0][n].start()
    for k in range(1, CAP):
        for n in range(len(LIB_PEERS)):
            stage_tile(n, k)
    for cp in loads[1:]:
        cp.start()
    for k in range(CAP):
        slots[own_box[0], own_box[1], k] = lib_ref[asked_s[mine, mine, k]]
    return tables, waves


def w_part(ref, j):
    return ref.at[pl.ds(2 * j, 2)]


def step_kernel(
    x_hbm, g_hbm, gain_ref, w_hbm, lib_hbm, wanted, home,
    out_hbm, grad_hbm, wsum_ref, gsum_ref,
    req_ref, order_ref, g_ref, w_ref, lib_ref, load_sems,
    inv_ref, q_ref, dm_ref, mixed_ref, dsh_ref, kvs, tt_ref, at_ref, stage, slots,
    asked, asked_s, table_sems, tile_sems, gslots, gsend, grecv, pair_sems, free_sem,
    store_sems, *piece_bufs,
):
    me = my_coords()
    pairs = [(lib_hbm, lib_ref), (x_hbm, dsh_ref), (w_part(w_hbm, 0), w_part(w_ref, 0)), (g_hbm, g_ref)]
    pairs += [(w_part(w_hbm, j), w_part(w_ref, j)) for j in (3, 1, 2)]
    loads = [pltpu.make_async_copy(a, b, load_sems.at[n]) for n, (a, b) in enumerate(pairs)]
    loads[0].start()

    barrier = pltpu.get_barrier_semaphore()
    peers = [lib_peer(me, dx, dc) for dx, dc in LIB_PEERS]
    peers += [{**me, a: along(me, a, s)} for a in ("y", "z") for s in (1, 2, 3)]
    for at in peers:
        pl.semaphore_signal(barrier, inc=1, device_id=device_of(at), device_id_type=MESH)
    req_ref[...] = request_table(wanted, home, order_ref)
    pl.semaphore_wait(barrier, len(peers))

    tables, waves = start_fetch(
        me, req_ref, lib_ref, loads, asked, asked_s, stage, slots, table_sems, tile_sems
    )

    def matrix(j):
        return w_part(w_ref, j)[...].reshape(D, D)

    for cp in loads[1:5]:
        cp.wait()

    @pl.loop(0, 2)
    def _(s):
        rows = pl.ds(pl.multiple_of(s * SEQ, SEQ), SEQ)
        x = dsh_ref[rows].astype(F32)
        inv = lax.rsqrt(jnp.mean(x * x, axis=1, keepdims=True) + EPSILON)
        inv_ref[rows] = inv
        normed = (x * inv * gain_ref[...]).astype(BF16)
        at_ref[0, :, rows] = normed.T
        q_ref[rows] = shift_up_rows(dot(normed, matrix(0))).astype(BF16)
        dm_ref[rows] = shift_up_rows(dot(g_ref[rows], matrix(3), ((1,), (1,)))).astype(BF16)

    for cp in loads[5:]:
        cp.wait()

    for k in range(CAP):
        for n in range(len(LIB_PEERS)):
            waves[k][n].wait_send()
            if k + 1 < CAP:
                waves[k + 1][n].start()
        for cp in waves[k]:
            cp.wait_recv()

        @pl.loop(0, 2)
        def _(h):
            t = slots[h, :, k].reshape(512, D)
            for half in range(2):
                c = slice(half * 512, half * 512 + 512)
                for m in range(2):
                    w = w_part(w_ref, 1 + m)[:, :, :, :, c].reshape(D, 512)
                    rows = dot(t, w).astype(BF16)
                    for o in range(4):
                        tile = rows[o * 128 : o * 128 + 128].reshape(4, 32, 512)
                        kvs[m, h * 16 + o * CAP + k, :, :, c] = tile

    pl.semaphore_signal(free_sem, inc=1, device_id=moved(me, "c", 1), device_id_type=MESH)

    @pl.loop(0, 16)
    def _(i):
        o = order_ref[i]
        t = slots[lax.div(o, 16), lax.rem(lax.div(o, 4), 4), lax.rem(o, 4)].reshape(128, D)
        tt_ref[:, pl.ds(pl.multiple_of(i * 128, 128), 128)] = t.T

    @pl.loop(0, 8)
    def _(b):
        attend(b, order_ref, q_ref, kvs.at[0], kvs.at[1], lib_ref, mixed_ref)

    @pl.loop(0, 2)
    def _(s):
        rows = pl.ds(pl.multiple_of(s * SEQ, SEQ), SEQ)
        attn = shift_down_rows(mixed_ref[rows].astype(F32)).astype(BF16)
        mixed_ref[rows] = attn
        at_ref[1, :, rows] = attn.T

    for cp in tables:
        cp.wait_send()

    def weight_terms(p):
        cols = slice(p * 256, p * 256 + 256)

        for j in range(4):
            for z in range(4):
                rows = slice(z * 256, z * 256 + 256)
                if j == 0:
                    res = dot(at_ref[0, rows, :], dsh_ref[:, cols])
                elif j == 3:
                    res = dot(at_ref[1, rows, :], g_ref[:, cols])
                else:
                    res = dot(tt_ref[rows, :], slots[j - 1, :, :, :, :, cols].reshape(2048, 256))
                res = res.astype(BF16)
                for xi in range(4):
                    for ci in range(2):
                        r0 = (xi * 2 + ci) * 32
                        stage[ci, j, z, xi, :, cols] = res[r0 : r0 + 32]

    def back(g):
        @pl.loop(0, 2)
        def _(b):
            attend_back(
                b * 4, 4, g, order_ref, q_ref, dm_ref, kvs.at[0], kvs.at[1], lib_ref, slots, dsh_ref
            )

        for s in range(2):
            at = (pl.ds(s * SEQ, SEQ), slice(g * 256, g * 256 + 256))
            dsh_ref[at] = shift_down_rows(dsh_ref[at].astype(F32)).astype(BF16)

    stores = []

    def store(src, dst, rows):
        n = len(stores)
        stores.append(pltpu.make_async_copy(src.at[rows], dst.at[rows], store_sems.at[n]))
        stores[n].start()

    def out_rows(s):
        rows = pl.ds(s * SEQ, SEQ)
        x = q_ref[rows].astype(F32)
        mixed_ref[rows] = (x + dot(mixed_ref[rows], matrix(3))).astype(BF16)
        store(mixed_ref, out_hbm, rows)

    def grad_rows(s):
        rows = pl.ds(s * SEQ, SEQ)
        x = q_ref[rows].astype(F32)
        inv = inv_ref[rows]
        dn = dot(dsh_ref[rows], matrix(0), ((1,), (1,)))
        dnx = dn * x * inv
        term = jnp.sum(dnx, axis=0, keepdims=True)
        gslots[0] = term if s == 0 else gslots[0] + term
        dh = dn * gain_ref[...]
        inner = jnp.mean(dh * x, axis=1, keepdims=True)
        dx = inv * dh - x * (inv * inv * inv) * inner
        dsh_ref[rows] = (g_ref[rows].astype(F32) + dx).astype(BF16)
        store(dsh_ref, grad_hbm, rows)

    sent = []
    paired = w_ref.at[pl.ds(2, 4)]
    n_each = len(piece_bufs) // (2 * PARTS)
    pair = {}
    flow = {}

    def send_part(p):
        if p == 0:
            pl.semaphore_wait(free_sem, 1)
        pair[p] = start_pair(me, p, stage, paired, pair_sems)
        sent.append(pair[p])

    def sum_part(p):
        end_pair(me, p, stage, paired, pair[p])
        flow[p] = []
        for h in range(2):
            q = 2 * p + h
            bufs = piece_bufs[q * n_each : (q + 1) * n_each]
            data = paired.at[:, :, :, :, pl.ds(q * 128, 128)]
            flow[p].append(reduce_piece(me, q, data, bufs, wsum_ref, sent))
            next(flow[p][-1])

    def advance(p):
        for f in flow[p]:
            next(f, None)

    back(0)
    weight_terms(0)
    send_part(0)
    back(1)
    sum_part(0)
    weight_terms(1)
    send_part(1)
    back(2)
    sum_part(1)
    advance(0)
    weight_terms(2)
    send_part(2)
    back(3)
    x_again = pltpu.make_async_copy(x_hbm, q_ref, load_sems.at[7])
    x_again.start()
    sum_part(2)
    advance(1)
    advance(0)
    weight_terms(3)
    send_part(3)
    x_again.wait()
    out_rows(0)
    sum_part(3)
    grad_rows(0)
    grad_rows(1)
    gain_flow = reduce_gain(me, gslots, gsend, grecv, sent)
    next(gain_flow)
    advance(2)
    advance(1)
    advance(0)
    out_rows(1)
    advance(3)
    next(gain_flow)
    advance(2)
    advance(1)
    advance(3)
    next(gain_flow)
    advance(2)
    advance(3)
    next(gain_flow, None)
    for cp in sent:
        cp.wait_send()
    for cp in stores:
        cp.wait()
    index = lax.axis_index("dp") * 8 + lax.axis_index("lib")
    gsum_ref[...] = pltpu.roll(gslots[0], lax.rem(D - index * 8, D), 1)[:, :128]


def train_step(hidden, cot, gains, weights, library, neighbours, tile_home):
    rows5 = (2, 4, 4, 4, 32, D)
    scratch = [
        pltpu.VMEM((8, 128), jnp.int32),
        pltpu.SMEM((16,), jnp.int32),
        pltpu.VMEM((512, D), BF16),
        pltpu.VMEM((8, 4, 4, 32, D), BF16),
        pltpu.VMEM((16, 4, 32, D), BF16),
        pltpu.SemaphoreType.DMA((8,)),
        pltpu.VMEM((512, 1), F32),
        pltpu.VMEM((512, D), BF16),
        pltpu.VMEM((512, D), BF16),
        pltpu.VMEM((512, D), BF16),
        pltpu.VMEM((512, D), BF16),
        pltpu.VMEM((2, 32, 4, 32, D), BF16),
        pltpu.VMEM((D, 2048), BF16),
        pltpu.VMEM((2, D, 512), BF16),
        pltpu.VMEM(rows5, BF16),
        pltpu.VMEM(rows5, BF16),
        pltpu.VMEM((8, 8, 128), jnp.int32),
        pltpu.SMEM((8, 8, 128), jnp.int32),
        pltpu.SemaphoreType.DMA((2, 8)),
        pltpu.SemaphoreType.DMA((2, 28)),
        pltpu.VMEM((17, 1, D), F32),
        pltpu.SemaphoreType.DMA((13,)),
        pltpu.SemaphoreType.DMA((13,)),
        pltpu.SemaphoreType.DMA((2, PARTS)),
        pltpu.SemaphoreType.REGULAR,
        pltpu.SemaphoreType.DMA((4,)),
    ]
    for _ in range(2 * PARTS):
        scratch += piece_scratch()
    hbm = pl.BlockSpec(memory_space=pl.ANY)
    smem = pl.BlockSpec(memory_space=pltpu.SMEM)
    vmem = pl.BlockSpec(memory_space=pltpu.VMEM)
    return pl.pallas_call(
        step_kernel,
        out_shape=(
            jax.ShapeDtypeStruct((512, D), BF16),
            jax.ShapeDtypeStruct((512, D), BF16),
            jax.ShapeDtypeStruct((32, D), F32),
            jax.ShapeDtypeStruct((1, 128), F32),
        ),
        in_specs=[hbm, hbm, vmem, hbm, hbm, smem, smem],
        out_specs=(hbm, hbm, vmem, vmem),
        scratch_shapes=scratch,
        compiler_params=pltpu.CompilerParams(
            collective_id=1, has_side_effects=True, vmem_limit_bytes=67000000
        ),
        name="train_step",
    )(hidden, cot, gains, weights.reshape(8, 4, 4, 32, D), library.reshape(16, 4, 32, D), neighbours, tile_home)


def hand_over_kernel(out_in, grad_in, w_in, g_in, out_ref, grad_ref, w_ref, g_ref, sems):
    copies = []
    for src, dst, n in ((out_in, out_ref, 4), (grad_in, grad_ref, 4), (w_in, w_ref, 1)):
        rows = src.shape[0] // n
        for k in range(n):
            part = pl.ds(k * rows, rows)
            copies.append(
                pltpu.make_async_copy(src.at[part], dst.at[part], sems.at[len(copies)])
            )
            copies[-1].start()
    g_ref[...] = g_in[0, :8]
    for cp in copies:
        cp.wait()


def hand_over(out, grad, w_share, g_sum):
    hbm = pl.BlockSpec(memory_space=pl.ANY)
    vmem = pl.BlockSpec(memory_space=pltpu.VMEM)
    return pl.pallas_call(
        hand_over_kernel,
        out_shape=(
            jax.ShapeDtypeStruct(out.shape, out.dtype),
            jax.ShapeDtypeStruct(grad.shape, grad.dtype),
            jax.ShapeDtypeStruct(w_share.shape, w_share.dtype),
            jax.ShapeDtypeStruct((8,), F32),
        ),
        in_specs=[vmem] * 4,
        out_specs=(hbm, hbm, hbm, vmem),
        scratch_shapes=[pltpu.SemaphoreType.DMA((9,))],
        name="hand_over",
    )(out, grad, w_share, g_sum)


def body(hidden_in, cotangent, gains, weights, library, neighbours, tile_home):
    results = train_step(
        hidden_in, cotangent, gains, weights[0], library, neighbours, tile_home
    )
    return hand_over(*results)


def solution(mesh):
    return jax.shard_map(
        body,
        mesh=mesh,
        in_specs=(
            P(("dp", "lib"), None),
            P(("dp", "lib"), None),
            P(),
            P(),
            P(("dp", "lib"), None, None),
            P(("dp", "lib"), None),
            P("dp", None),
        ),
        out_specs=(
            P(("dp", "lib"), None),
            P(("dp", "lib"), None),
            P(("dp", "lib"), None),
            P(("dp", "lib")),
        ),
        check_vma=False,
    )
```

```python
import functools

import jax
import jax.numpy as jnp
from jax import lax
from jax.experimental import pallas as pl
from jax.experimental.pallas import tpu as pltpu
from jax.sharding import PartitionSpec as P

HD = 64
BLOCK = 64
CAP = 4
SEQ = 256
D = 1024
EPSILON = 1e-06

F32 = jnp.float32
BF16 = jnp.bfloat16
MESH = pl.DeviceIdType.MESH

ORDERS = (
    ("x", "y", "z"),
    ("y", "z", "x"),
    ("z", "x", "y"),
    ("x", "z", "y"),
    ("y", "x", "z"),
    ("z", "y", "x"),
    ("x", "y", "z"),
    ("z", "x", "y"),
)
PARTS = 4
DIMS = ("y", "z", "x")


def dot(left, right, dims=((1,), (0,))):
    return lax.dot_general(left, right, (dims, ((), ())), preferred_element_type=F32)


def my_coords():
    dp = lax.axis_index("dp")
    lib = lax.axis_index("lib")
    return {
        "y": lax.div(dp, 4),
        "z": lax.rem(dp, 4),
        "x": lax.div(lib, 2),
        "c": lax.rem(lib, 2),
    }


def device_of(at):
    return (at["y"] * 4 + at["z"], at["x"] * 2 + at["c"])


def along(me, axis, step):
    size = 2 if axis == "c" else 4
    return lax.rem(me[axis] + step, size)


def moved(me, axis, step):
    return device_of({**me, axis: along(me, axis, step)})


def piece_scratch():
    shapes = []
    for left in (2, 1, 0):
        block = (4,) * left + (32, 128)
        shapes.append(pltpu.VMEM((3,) + block, BF16))
    shapes.append(pltpu.SemaphoreType.DMA((2, 9)))
    return shapes


def start_pair(me, p, j, own, paired, sems):
    cols = slice(p * 256, p * 256 + 256)
    cp = pltpu.make_async_remote_copy(
        src_ref=own.at[along(me, "c", 1), j, :, :, :, cols],
        dst_ref=paired.at[j, :, :, :, cols],
        send_sem=sems.at[0, p * 4 + j],
        recv_sem=sems.at[1, p * 4 + j],
        device_id=moved(me, "c", 1),
        device_id_type=MESH,
    )
    cp.start()
    return cp


def end_pair(me, p, own, paired, copies):
    cols = slice(p * 256, p * 256 + 256)
    for j, cp in copies:
        cp.wait_recv()

        @pl.loop(0, 4)
        def _(z):
            total = own[me["c"], j, z, :, :, cols].astype(F32)
            total = total + paired[j, z, :, :, cols].astype(F32)
            paired[j, z, :, :, cols] = total.astype(BF16)


def reduce_piece(me, q, data, bufs, w_out, sent):
    sems = bufs[-1]
    dims = list(DIMS)
    n = 0
    for pos, axis in enumerate(ORDERS[q]):
        recv = bufs[pos]
        at = dims.index(axis)

        def chunk(step):
            idx = [slice(None)] * len(dims)
            idx[at] = along(me, axis, step)
            return tuple(idx)

        cps = []
        for step in (2, 1, 3):
            cp = pltpu.make_async_remote_copy(
                src_ref=data.at[chunk(step)],
                dst_ref=recv.at[step - 1],
                send_sem=sems.at[0, n],
                recv_sem=sems.at[1, n],
                device_id=moved(me, axis, step),
                device_id_type=MESH,
            )
            cp.start()
            sent.append(cp)
            cps.append(cp)
            n += 1
        yield
        for cp in cps:
            cp.wait_recv()
        total = data[chunk(0)].astype(F32)
        for k in range(3):
            total = total + recv[k].astype(F32)
        if pos < 2:
            data = recv.at[0]
            data[...] = total.astype(BF16)
        else:
            w_out[:, q * 128 : q * 128 + 128] = total
        dims.remove(axis)


def reduce_gain(me, slots, send_sem, recv_sem, sent):
    k = 0
    for stage, axis in enumerate(("lib", "y", "z"), 1):
        if axis == "lib":
            peers = [lib_peer(me, dx, dc) for dx, dc in LIB_PEERS]
        else:
            peers = [{**me, axis: along(me, axis, step)} for step in (1, 2, 3)]
        slots[stage] = slots[0]
        cps = []
        first = k
        for at in peers:
            cp = pltpu.make_async_remote_copy(
                src_ref=slots.at[stage],
                dst_ref=slots.at[4 + k],
                send_sem=send_sem.at[k],
                recv_sem=recv_sem.at[k],
                device_id=device_of(at),
                device_id_type=MESH,
            )
            cp.start()
            sent.append(cp)
            cps.append(cp)
            k += 1
        yield
        total = slots[stage]
        for i, cp in enumerate(cps):
            cp.wait_recv()
            total = total + slots[4 + first + i]
        slots[0] = total


def shift_up_rows(rows):
    moved_rows = pltpu.roll(rows, SEQ - (BLOCK - 1), 0)
    row = lax.broadcasted_iota(jnp.int32, rows.shape, 0)
    return jnp.where(row < SEQ - BLOCK + 1, moved_rows, 0.0)


def shift_down_rows(rows):
    moved_rows = pltpu.roll(rows, BLOCK - 1, 0)
    row = lax.broadcasted_iota(jnp.int32, rows.shape, 0)
    return jnp.where(row >= BLOCK - 1, moved_rows, 0.0)


def head_of(shape, dim):
    return lax.broadcasted_iota(jnp.int32, shape, dim) // HD


def spread(rows):
    same = head_of((256, 256), 0) == head_of((256, 256), 1)
    return jnp.where(same, jnp.concatenate([rows] * 4, axis=0), jnp.zeros((), BF16))


def diag(full):
    hcol = head_of((64, 256), 1)
    out = full[0:64]
    for h in range(1, 4):
        out = jnp.where(hcol == h, full[h * 64 : h * 64 + 64], out)
    return out


def block_rows(b):
    return pl.ds(pl.multiple_of(b * 64, 64), 64)


def block_tiles(b):
    return lax.div(b, 2), pl.ds(lax.rem(b, 2) * 2, 2)


def slot_rows(ref, order_ref, b, c):
    tiles = [ref[order_ref[b * 2 + n], :, :, c].reshape(128, 256) for n in range(2)]
    return jnp.concatenate(tiles, axis=0)


def attend(b, order_ref, q_ref, k_ref, v_ref, prob_ref, mixed_ref):
    groups = [slice(g * 256, g * 256 + 256) for g in range(4)]
    rows = block_rows(b)
    qbd = [spread(q_ref[rows, c]) for c in groups]
    keys = [slot_rows(k_ref, order_ref, b, c) for c in groups]
    vals = [slot_rows(v_ref, order_ref, b, c) for c in groups]
    score = [dot(k, q, ((1,), (1,))) * HD ** (-0.5) for k, q in zip(keys, qbd)]
    e = [jnp.exp(a - jnp.max(a, axis=0, keepdims=True)) for a in score]
    pb = [(a * (1.0 / jnp.sum(a, axis=0, keepdims=True))).astype(BF16) for a in e]
    mixed = [diag(dot(a, v, ((0,), (0,)))).astype(BF16) for a, v in zip(pb, vals)]
    for g, c in enumerate(groups):
        prob_ref[pl.ds(b * 2, 2), :, :, c] = pb[g].reshape(2, 4, 32, 256)
        mixed_ref[rows, c] = mixed[g]


def attend_back(b0, n_blocks, g, order_ref, q_ref, dm_ref, k_ref, v_ref, prob_ref, dkv_ref, dsh_ref):
    c = slice(g * 256, g * 256 + 256)
    blocks = [b0 + k for k in range(n_blocks)]
    at = [block_tiles(b) for b in blocks]
    qbd = [spread(q_ref[block_rows(b), c]) for b in blocks]
    dobd = [spread(dm_ref[block_rows(b), c]) for b in blocks]
    keys = [slot_rows(k_ref, order_ref, b, c) for b in blocks]
    vals = [slot_rows(v_ref, order_ref, b, c) for b in blocks]
    pb = [prob_ref[pl.ds(b * 2, 2), :, :, c].reshape(256, 256) for b in blocks]
    dp = [dot(v, d, ((1,), (1,))) for v, d in zip(vals, dobd)]
    dv = [dot(a, d).astype(BF16).reshape(2, 4, 32, 256) for a, d in zip(pb, dobd)]
    p = [a.astype(F32) for a in pb]
    pdp = [a * d for a, d in zip(p, dp)]
    rd = [
        jnp.sum(w, axis=0, keepdims=True) * (1.0 / jnp.sum(a, axis=0, keepdims=True))
        for w, a in zip(pdp, p)
    ]
    ds = [((w - a * r) * HD ** (-0.5)).astype(BF16) for w, a, r in zip(pdp, p, rd)]
    dsh = [diag(dot(a, k, ((0,), (0,)))).astype(BF16) for a, k in zip(ds, keys)]
    dk = [dot(a, q).astype(BF16).reshape(2, 4, 32, 256) for a, q in zip(ds, qbd)]
    for k, b in enumerate(blocks):
        i, n = at[k]
        dsh_ref[block_rows(b), c] = dsh[k]
        dkv_ref[1, i, n, :, :, c] = dv[k]
        dkv_ref[0, i, n, :, :, c] = dk[k]


LIB_PEERS = ((2, 0), (2, 1), (1, 0), (3, 0), (1, 1), (3, 1), (0, 1))


def lib_peer(me, dx, dc):
    return {**me, "x": along(me, "x", dx), "c": along(me, "c", dc)}


def request_table(wanted, home, order):
    row = lax.broadcasted_iota(jnp.int32, (8, 128), 0)
    col = lax.broadcasted_iota(jnp.int32, (8, 128), 1)
    table = jnp.zeros((8, 128), jnp.int32)
    owners = []
    for i in range(16):
        stored = home[0, wanted[i % 2, i // 2]]
        owner = lax.div(stored, 16)
        rank = jnp.int32(0)
        for before in owners:
            rank = rank + jnp.where(before == owner, 1, 0)
        owners.append(owner)
        order[i] = owner * CAP + rank
        table = jnp.where((row == owner) & (col == rank), lax.rem(stored, 16), table)
    return table.reshape(8, 1, 128)


def start_fetch(me, req_ref, lib_ref, loads, asked, asked_s, stage, slots, table_sems, tile_sems):
    mine = me["x"] * 2 + me["c"]
    tables = []
    for n, (dx, dc) in enumerate(LIB_PEERS):
        at = lib_peer(me, dx, dc)
        cp = pltpu.make_async_remote_copy(
            src_ref=req_ref.at[at["x"] * 2 + at["c"]],
            dst_ref=asked.at[mine],
            send_sem=table_sems.at[0, n],
            recv_sem=table_sems.at[1, n],
            device_id=device_of(at),
            device_id_type=MESH,
        )
        cp.start()
        tables.append(cp)
    asked[mine] = req_ref[mine]
    for cp in tables:
        cp.wait_recv()
    local = pltpu.make_async_copy(asked, asked_s, table_sems.at[0, 7])
    local.start()
    local.wait()
    loads[0].wait()
    own_box = (lax.div(mine, 4), lax.rem(mine, 4))
    waves = []
    for k in range(CAP):
        wave = []
        for n, (dx, dc) in enumerate(LIB_PEERS):
            cp = pltpu.make_async_remote_copy(
                src_ref=stage.at[n // 4, n % 4, k],
                dst_ref=slots.at[own_box[0], own_box[1], k],
                send_sem=tile_sems.at[0, n * CAP + k],
                recv_sem=tile_sems.at[1, n * CAP + k],
                device_id=device_of(lib_peer(me, dx, dc)),
                device_id_type=MESH,
            )
            wave.append(cp)
        waves.append(wave)

    def stage_tile(n, k):
        at = lib_peer(me, *LIB_PEERS[n])
        peer = at["x"] * 2 + at["c"]
        stage[n // 4, n % 4, k] = lib_ref[asked_s[peer, 0, k]]

    for n in range(len(LIB_PEERS)):
        stage_tile(n, 0)
        waves[0][n].start()
    for k in range(1, CAP):
        for n in range(len(LIB_PEERS)):
            stage_tile(n, k)
    for cp in loads[1:]:
        cp.start()
    for k in range(CAP):
        slots[own_box[0], own_box[1], k] = lib_ref[asked_s[mine, 0, k]]
    return tables, waves


def w_part(ref, j):
    return ref.at[pl.ds(2 * j, 2)]


def step_kernel(
    x_hbm, g_hbm, gain_ref, w_hbm, lib_hbm, wanted, home,
    out_hbm, grad_hbm, wsum_ref, gsum_ref,
    req_ref, order_ref, g_ref, w_ref, lib_ref, load_sems,
    inv_ref, q_ref, dm_ref, mixed_ref, dsh_ref, kvs, tt_ref, at_ref, stage, slots,
    asked, asked_s, table_sems, tile_sems, gslots, gsend, grecv, pair_sems, free_sem,
    store_sems, *piece_bufs,
):
    me = my_coords()
    pairs = [(lib_hbm, lib_ref), (x_hbm, dsh_ref), (w_part(w_hbm, 0), w_part(w_ref, 0)), (g_hbm, g_ref)]
    pairs += [(w_part(w_hbm, j), w_part(w_ref, j)) for j in (3, 1, 2)]
    loads = [pltpu.make_async_copy(a, b, load_sems.at[n]) for n, (a, b) in enumerate(pairs)]
    loads[0].start()

    barrier = pltpu.get_barrier_semaphore()
    peers = [lib_peer(me, dx, dc) for dx, dc in LIB_PEERS]
    peers += [{**me, a: along(me, a, s)} for a in ("y", "z") for s in (1, 2, 3)]
    for at in peers:
        pl.semaphore_signal(barrier, inc=1, device_id=device_of(at), device_id_type=MESH)
    req_ref[...] = request_table(wanted, home, order_ref)
    pl.semaphore_wait(barrier, len(peers))

    tables, waves = start_fetch(
        me, req_ref, lib_ref, loads, asked, asked_s, stage, slots, table_sems, tile_sems
    )

    def matrix(j):
        return w_part(w_ref, j)[...].reshape(D, D)

    for cp in loads[1:5]:
        cp.wait()

    @pl.loop(0, 2)
    def _(s):
        rows = pl.ds(pl.multiple_of(s * SEQ, SEQ), SEQ)
        x = dsh_ref[rows].astype(F32)
        inv = lax.rsqrt(jnp.mean(x * x, axis=1, keepdims=True) + EPSILON)
        inv_ref[rows] = inv
        normed = (x * inv * gain_ref[...]).astype(BF16)
        at_ref[0, :, rows] = normed.T
        q_ref[rows] = shift_up_rows(dot(normed, matrix(0))).astype(BF16)
        dm_ref[rows] = shift_up_rows(dot(g_ref[rows], matrix(3), ((1,), (1,)))).astype(BF16)

    for cp in loads[5:]:
        cp.wait()

    for k in range(CAP):
        for n in range(len(LIB_PEERS)):
            waves[k][n].wait_send()
            if k + 1 < CAP:
                waves[k + 1][n].start()
        for dx in (0, 1):
            for n, (px, _) in enumerate(LIB_PEERS):
                if px % 2 == dx:
                    waves[k][n].wait_recv()
            chips = [along(me, "x", dx), along(me, "x", dx + 2)]
            t = [slots[lax.div(c, 2), pl.ds(lax.rem(c, 2) * 2, 2), k] for c in chips]
            t = jnp.concatenate([a.reshape(256, D) for a in t], axis=0)
            for half in range(2):
                c = slice(half * 512, half * 512 + 512)
                for m in range(2):
                    w = w_part(w_ref, 1 + m)[:, :, :, :, c].reshape(D, 512)
                    rows = dot(t, w).astype(BF16)
                    for o in range(4):
                        tile = rows[o * 128 : o * 128 + 128].reshape(4, 32, 512)
                        kvs[m, (chips[o // 2] * 2 + o % 2) * CAP + k, :, :, c] = tile

    pl.semaphore_signal(free_sem, inc=1, device_id=moved(me, "c", 1), device_id_type=MESH)

    @pl.loop(0, 16)
    def _(i):
        o = order_ref[i]
        t = slots[lax.div(o, 16), lax.rem(lax.div(o, 4), 4), lax.rem(o, 4)].reshape(128, D)
        tt_ref[:, pl.ds(pl.multiple_of(i * 128, 128), 128)] = t.T

    @pl.loop(0, 8, unroll=2)
    def _(b):
        attend(b, order_ref, q_ref, kvs.at[0], kvs.at[1], lib_ref, mixed_ref)

    @pl.loop(0, 2)
    def _(s):
        rows = pl.ds(pl.multiple_of(s * SEQ, SEQ), SEQ)
        attn = shift_down_rows(mixed_ref[rows].astype(F32)).astype(BF16)
        mixed_ref[rows] = attn
        at_ref[1, :, rows] = attn.T

    for cp in tables:
        cp.wait_send()

    sent = []
    pair = {}
    paired = w_ref.at[pl.ds(2, 4)]

    def weight_terms(p):
        cols = slice(p * 256, p * 256 + 256)
        pair[p] = []
        for j in (1, 2, 0, 3):
            for z in range(4):
                rows = slice(z * 256, z * 256 + 256)
                if j == 0:
                    res = dot(at_ref[0, rows, :], dsh_ref[:, cols])
                elif j == 3:
                    res = dot(at_ref[1, rows, :], g_ref[:, cols])
                else:
                    res = dot(tt_ref[rows, :], slots[j - 1, :, :, :, :, cols].reshape(2048, 256))
                res = res.astype(BF16)
                for xi in range(4):
                    for ci in range(2):
                        r0 = (xi * 2 + ci) * 32
                        stage[ci, j, z, xi, :, cols] = res[r0 : r0 + 32]
            if p == 0 and not pair[p]:
                pl.semaphore_wait(free_sem, 1)
            cp = start_pair(me, p, j, stage, paired, pair_sems)
            sent.append(cp)
            pair[p].append((j, cp))

    def back(g):
        @pl.loop(0, 2)
        def _(b):
            attend_back(
                b * 4, 4, g, order_ref, q_ref, dm_ref, kvs.at[0], kvs.at[1], lib_ref, slots, dsh_ref
            )

        for s in range(2):
            at = (pl.ds(s * SEQ, SEQ), slice(g * 256, g * 256 + 256))
            dsh_ref[at] = shift_down_rows(dsh_ref[at].astype(F32)).astype(BF16)

    stores = []

    def store(src, dst, rows):
        n = len(stores)
        stores.append(pltpu.make_async_copy(src.at[rows], dst.at[rows], store_sems.at[n]))
        stores[n].start()

    def out_rows(s):
        rows = pl.ds(s * SEQ, SEQ)
        x = q_ref[rows].astype(F32)
        mixed_ref[rows] = (x + dot(mixed_ref[rows], matrix(3))).astype(BF16)
        store(mixed_ref, out_hbm, rows)

    def grad_rows(s):
        rows = pl.ds(s * SEQ, SEQ)
        x = q_ref[rows].astype(F32)
        inv = inv_ref[rows]
        dn = dot(dsh_ref[rows], matrix(0), ((1,), (1,)))
        dnx = dn * x * inv
        term = jnp.sum(dnx, axis=0, keepdims=True)
        gslots[0] = term if s == 0 else gslots[0] + term
        dh = dn * gain_ref[...]
        inner = jnp.mean(dh * x, axis=1, keepdims=True)
        dx = inv * dh - x * (inv * inv * inv) * inner
        dsh_ref[rows] = (g_ref[rows].astype(F32) + dx).astype(BF16)
        store(dsh_ref, grad_hbm, rows)

    n_each = len(piece_bufs) // (2 * PARTS)
    flow = {}

    def sum_part(p):
        end_pair(me, p, stage, paired, pair[p])
        flow[p] = []
        for h in range(2):
            q = 2 * p + h
            bufs = piece_bufs[q * n_each : (q + 1) * n_each]
            data = paired.at[:, :, :, :, pl.ds(q * 128, 128)]
            flow[p].append(reduce_piece(me, q, data, bufs, wsum_ref, sent))
            next(flow[p][-1])

    def advance(p):
        for f in flow[p]:
            next(f, None)

    back(0)
    weight_terms(0)
    back(1)
    sum_part(0)
    weight_terms(1)
    back(2)
    sum_part(1)
    advance(0)
    weight_terms(2)
    back(3)
    x_again = pltpu.make_async_copy(x_hbm, q_ref, load_sems.at[7])
    x_again.start()
    sum_part(2)
    advance(1)
    advance(0)
    weight_terms(3)
    x_again.wait()
    out_rows(0)
    sum_part(3)
    grad_rows(0)
    grad_rows(1)
    gain_flow = reduce_gain(me, gslots, gsend, grecv, sent)
    next(gain_flow)
    advance(2)
    advance(1)
    advance(0)
    out_rows(1)
    advance(3)
    next(gain_flow)
    advance(2)
    advance(1)
    advance(3)
    next(gain_flow)
    advance(2)
    advance(3)
    next(gain_flow, None)
    for cp in sent:
        cp.wait_send()
    for cp in stores:
        cp.wait()
    index = lax.axis_index("dp") * 8 + lax.axis_index("lib")
    gsum_ref[...] = pltpu.roll(gslots[0], lax.rem(D - index * 8, D), 1)[:, :128]


def train_step(hidden, cot, gains, weights, library, neighbours, tile_home):
    rows5 = (2, 4, 4, 4, 32, D)
    scratch = [
        pltpu.VMEM((8, 1, 128), jnp.int32),
        pltpu.SMEM((16,), jnp.int32),
        pltpu.VMEM((512, D), BF16),
        pltpu.VMEM((8, 4, 4, 32, D), BF16),
        pltpu.VMEM((16, 4, 32, D), BF16),
        pltpu.SemaphoreType.DMA((8,)),
        pltpu.VMEM((512, 1), F32),
        pltpu.VMEM((512, D), BF16),
        pltpu.VMEM((512, D), BF16),
        pltpu.VMEM((512, D), BF16),
        pltpu.VMEM((512, D), BF16),
        pltpu.VMEM((2, 32, 4, 32, D), BF16),
        pltpu.VMEM((D, 2048), BF16),
        pltpu.VMEM((2, D, 512), BF16),
        pltpu.VMEM(rows5, BF16),
        pltpu.VMEM(rows5, BF16),
        pltpu.VMEM((8, 1, 128), jnp.int32),
        pltpu.SMEM((8, 1, 128), jnp.int32),
        pltpu.SemaphoreType.DMA((2, 8)),
        pltpu.SemaphoreType.DMA((2, 28)),
        pltpu.VMEM((17, 1, D), F32),
        pltpu.SemaphoreType.DMA((13,)),
        pltpu.SemaphoreType.DMA((13,)),
        pltpu.SemaphoreType.DMA((2, 4 * PARTS)),
        pltpu.SemaphoreType.REGULAR,
        pltpu.SemaphoreType.DMA((4,)),
    ]
    for _ in range(2 * PARTS):
        scratch += piece_scratch()
    hbm = pl.BlockSpec(memory_space=pl.ANY)
    smem = pl.BlockSpec(memory_space=pltpu.SMEM)
    vmem = pl.BlockSpec(memory_space=pltpu.VMEM)
    return pl.pallas_call(
        step_kernel,
        out_shape=(
            jax.ShapeDtypeStruct((512, D), BF16),
            jax.ShapeDtypeStruct((512, D), BF16),
            jax.ShapeDtypeStruct((32, D), F32),
            jax.ShapeDtypeStruct((1, 128), F32),
        ),
        in_specs=[hbm, hbm, vmem, hbm, hbm, smem, smem],
        out_specs=(hbm, hbm, vmem, vmem),
        scratch_shapes=scratch,
        compiler_params=pltpu.CompilerParams(
            collective_id=1, has_side_effects=True, vmem_limit_bytes=67000000
        ),
        name="train_step",
    )(hidden, cot, gains, weights.reshape(8, 4, 4, 32, D), library.reshape(16, 4, 32, D), neighbours.T, tile_home)


def hand_over_kernel(out_in, grad_in, w_in, g_in, out_ref, grad_ref, w_ref, g_ref, sems):
    copies = []
    for src, dst, n in ((out_in, out_ref, 4), (grad_in, grad_ref, 4), (w_in, w_ref, 1)):
        rows = src.shape[0] // n
        for k in range(n):
            part = pl.ds(k * rows, rows)
            copies.append(
                pltpu.make_async_copy(src.at[part], dst.at[part], sems.at[len(copies)])
            )
            copies[-1].start()
    g_ref[...] = g_in[0, :8]
    for cp in copies:
        cp.wait()


def hand_over(out, grad, w_share, g_sum):
    hbm = pl.BlockSpec(memory_space=pl.ANY)
    vmem = pl.BlockSpec(memory_space=pltpu.VMEM)
    return pl.pallas_call(
        hand_over_kernel,
        out_shape=(
            jax.ShapeDtypeStruct(out.shape, out.dtype),
            jax.ShapeDtypeStruct(grad.shape, grad.dtype),
            jax.ShapeDtypeStruct(w_share.shape, w_share.dtype),
            jax.ShapeDtypeStruct((8,), F32),
        ),
        in_specs=[vmem] * 4,
        out_specs=(hbm, hbm, hbm, vmem),
        scratch_shapes=[pltpu.SemaphoreType.DMA((9,))],
        name="hand_over",
    )(out, grad, w_share, g_sum)


def body(hidden_in, cotangent, gains, weights, library, neighbours, tile_home):
    results = train_step(
        hidden_in, cotangent, gains, weights[0], library, neighbours, tile_home
    )
    return hand_over(*results)


def solution(mesh):
    return jax.shard_map(
        body,
        mesh=mesh,
        in_specs=(
            P(("dp", "lib"), None),
            P(("dp", "lib"), None),
            P(),
            P(),
            P(("dp", "lib"), None, None),
            P(("dp", "lib"), None),
            P("dp", None),
        ),
        out_specs=(
            P(("dp", "lib"), None),
            P(("dp", "lib"), None),
            P(("dp", "lib"), None),
            P(("dp", "lib")),
        ),
        check_vma=False,
    )
```

```python
import functools

import jax
import jax.numpy as jnp
from jax import lax
from jax.experimental import pallas as pl
from jax.experimental.pallas import tpu as pltpu
from jax.sharding import PartitionSpec as P

HD = 64
BLOCK = 64
CAP = 4
SEQ = 256
D = 1024
EPSILON = 1e-06

F32 = jnp.float32
BF16 = jnp.bfloat16
MESH = pl.DeviceIdType.MESH

ORDERS = (
    ("x", "y", "z"),
    ("y", "z", "x"),
    ("z", "x", "y"),
    ("x", "z", "y"),
    ("y", "x", "z"),
    ("z", "y", "x"),
    ("x", "y", "z"),
    ("z", "x", "y"),
)
PARTS = 4
DIMS = ("y", "z", "x")


def dot(left, right, dims=((1,), (0,))):
    return lax.dot_general(left, right, (dims, ((), ())), preferred_element_type=F32)


def my_coords():
    dp = lax.axis_index("dp")
    lib = lax.axis_index("lib")
    return {
        "y": lax.div(dp, 4),
        "z": lax.rem(dp, 4),
        "x": lax.div(lib, 2),
        "c": lax.rem(lib, 2),
    }


def device_of(at):
    return (at["y"] * 4 + at["z"], at["x"] * 2 + at["c"])


def along(me, axis, step):
    size = 2 if axis == "c" else 4
    return lax.rem(me[axis] + step, size)


def moved(me, axis, step):
    return device_of({**me, axis: along(me, axis, step)})


def piece_scratch():
    shapes = []
    for left in (2, 1, 0):
        block = (4,) * left + (32, 128)
        shapes.append(pltpu.VMEM((3,) + block, BF16))
    shapes.append(pltpu.SemaphoreType.DMA((2, 9)))
    return shapes


def start_pair(me, p, j, own, paired, sems):
    cols = slice(p * 256, p * 256 + 256)
    cp = pltpu.make_async_remote_copy(
        src_ref=own.at[along(me, "c", 1), j, :, :, :, cols],
        dst_ref=paired.at[j, :, :, :, cols],
        send_sem=sems.at[0, p * 4 + j],
        recv_sem=sems.at[1, p * 4 + j],
        device_id=moved(me, "c", 1),
        device_id_type=MESH,
    )
    cp.start()
    return cp


def end_pair(me, p, own, paired, copies):
    cols = slice(p * 256, p * 256 + 256)
    for j, cp in copies:
        cp.wait_recv()

        @pl.loop(0, 4)
        def _(z):
            total = own[me["c"], j, z, :, :, cols].astype(F32)
            total = total + paired[j, z, :, :, cols].astype(F32)
            paired[j, z, :, :, cols] = total.astype(BF16)


def reduce_piece(me, q, data, bufs, w_out, sent):
    sems = bufs[-1]
    dims = list(DIMS)
    n = 0
    for pos, axis in enumerate(ORDERS[q]):
        recv = bufs[pos]
        at = dims.index(axis)

        def chunk(step):
            idx = [slice(None)] * len(dims)
            idx[at] = along(me, axis, step)
            return tuple(idx)

        cps = []
        for step in (2, 1, 3):
            cp = pltpu.make_async_remote_copy(
                src_ref=data.at[chunk(step)],
                dst_ref=recv.at[step - 1],
                send_sem=sems.at[0, n],
                recv_sem=sems.at[1, n],
                device_id=moved(me, axis, step),
                device_id_type=MESH,
            )
            cp.start()
            sent.append(cp)
            cps.append(cp)
            n += 1
        yield
        for cp in cps:
            cp.wait_recv()
        total = data[chunk(0)].astype(F32)
        for k in range(3):
            total = total + recv[k].astype(F32)
        if pos < 2:
            data = recv.at[0]
            data[...] = total.astype(BF16)
        else:
            w_out[:, q * 128 : q * 128 + 128] = total
        dims.remove(axis)


def reduce_gain(me, slots, send_sem, recv_sem, sent):
    k = 0
    for stage, axis in enumerate(("lib", "y", "z"), 1):
        if axis == "lib":
            peers = [lib_peer(me, dx, dc) for dx, dc in LIB_PEERS]
        else:
            peers = [{**me, axis: along(me, axis, step)} for step in (1, 2, 3)]
        slots[stage] = slots[0]
        cps = []
        first = k
        for at in peers:
            cp = pltpu.make_async_remote_copy(
                src_ref=slots.at[stage],
                dst_ref=slots.at[4 + k],
                send_sem=send_sem.at[k],
                recv_sem=recv_sem.at[k],
                device_id=device_of(at),
                device_id_type=MESH,
            )
            cp.start()
            sent.append(cp)
            cps.append(cp)
            k += 1
        yield
        total = slots[stage]
        for i, cp in enumerate(cps):
            cp.wait_recv()
            total = total + slots[4 + first + i]
        slots[0] = total


def shift_up_rows(rows):
    moved_rows = pltpu.roll(rows, SEQ - (BLOCK - 1), 0)
    row = lax.broadcasted_iota(jnp.int32, rows.shape, 0)
    return jnp.where(row < SEQ - BLOCK + 1, moved_rows, 0.0)


def shift_down_rows(rows):
    moved_rows = pltpu.roll(rows, BLOCK - 1, 0)
    row = lax.broadcasted_iota(jnp.int32, rows.shape, 0)
    return jnp.where(row >= BLOCK - 1, moved_rows, 0.0)


def head_of(shape, dim):
    return lax.broadcasted_iota(jnp.int32, shape, dim) // HD


def spread(rows):
    same = head_of((256, 256), 0) == head_of((256, 256), 1)
    return jnp.where(same, jnp.concatenate([rows] * 4, axis=0), jnp.zeros((), BF16))


def diag(full):
    hcol = head_of((64, 256), 1)
    out = full[0:64]
    for h in range(1, 4):
        out = jnp.where(hcol == h, full[h * 64 : h * 64 + 64], out)
    return out


def block_rows(b):
    return pl.ds(pl.multiple_of(b * 64, 64), 64)


def block_tiles(b):
    return lax.div(b, 2), pl.ds(lax.rem(b, 2) * 2, 2)


def slot_rows(ref, order_ref, b, c):
    tiles = [ref[order_ref[b * 2 + n], :, :, c].reshape(128, 256) for n in range(2)]
    return jnp.concatenate(tiles, axis=0)


def attend(b, order_ref, q_ref, k_ref, v_ref, prob_ref, mixed_ref):
    groups = [slice(g * 256, g * 256 + 256) for g in range(4)]
    rows = block_rows(b)
    qbd = [spread(q_ref[rows, c]) for c in groups]
    keys = [slot_rows(k_ref, order_ref, b, c) for c in groups]
    vals = [slot_rows(v_ref, order_ref, b, c) for c in groups]
    score = [dot(k, q, ((1,), (1,))) * HD ** (-0.5) for k, q in zip(keys, qbd)]
    e = [jnp.exp(a - jnp.max(a, axis=0, keepdims=True)) for a in score]
    pb = [(a * (1.0 / jnp.sum(a, axis=0, keepdims=True))).astype(BF16) for a in e]
    mixed = [diag(dot(a, v, ((0,), (0,)))).astype(BF16) for a, v in zip(pb, vals)]
    for g, c in enumerate(groups):
        prob_ref[pl.ds(b * 2, 2), :, :, c] = pb[g].reshape(2, 4, 32, 256)
        mixed_ref[rows, c] = mixed[g]


def attend_back(b0, n_blocks, g, order_ref, q_ref, dm_ref, k_ref, v_ref, prob_ref, dkv_ref, dsh_ref):
    c = slice(g * 256, g * 256 + 256)
    blocks = [b0 + k for k in range(n_blocks)]
    at = [block_tiles(b) for b in blocks]
    qbd = [spread(q_ref[block_rows(b), c]) for b in blocks]
    dobd = [spread(dm_ref[block_rows(b), c]) for b in blocks]
    keys = [slot_rows(k_ref, order_ref, b, c) for b in blocks]
    vals = [slot_rows(v_ref, order_ref, b, c) for b in blocks]
    pb = [prob_ref[pl.ds(b * 2, 2), :, :, c].reshape(256, 256) for b in blocks]
    dp = [dot(v, d, ((1,), (1,))) for v, d in zip(vals, dobd)]
    dv = [dot(a, d).astype(BF16).reshape(2, 4, 32, 256) for a, d in zip(pb, dobd)]
    p = [a.astype(F32) for a in pb]
    pdp = [a * d for a, d in zip(p, dp)]
    rd = [
        jnp.sum(w, axis=0, keepdims=True) * (1.0 / jnp.sum(a, axis=0, keepdims=True))
        for w, a in zip(pdp, p)
    ]
    ds = [((w - a * r) * HD ** (-0.5)).astype(BF16) for w, a, r in zip(pdp, p, rd)]
    dsh = [diag(dot(a, k, ((0,), (0,)))).astype(BF16) for a, k in zip(ds, keys)]
    dk = [dot(a, q).astype(BF16).reshape(2, 4, 32, 256) for a, q in zip(ds, qbd)]
    for k, b in enumerate(blocks):
        i, n = at[k]
        dsh_ref[block_rows(b), c] = dsh[k]
        dkv_ref[1, i, n, :, :, c] = dv[k]
        dkv_ref[0, i, n, :, :, c] = dk[k]


LIB_PEERS = ((2, 0), (2, 1), (1, 0), (3, 0), (1, 1), (3, 1), (0, 1))


def lib_peer(me, dx, dc):
    return {**me, "x": along(me, "x", dx), "c": along(me, "c", dc)}


def request_table(wanted, home, order):
    row = lax.broadcasted_iota(jnp.int32, (8, 128), 0)
    col = lax.broadcasted_iota(jnp.int32, (8, 128), 1)
    table = jnp.zeros((8, 128), jnp.int32)
    owners = []
    for i in range(16):
        stored = home[0, wanted[i % 2, i // 2]]
        owner = lax.div(stored, 16)
        rank = jnp.int32(0)
        for before in owners:
            rank = rank + jnp.where(before == owner, 1, 0)
        owners.append(owner)
        order[i] = owner * CAP + rank
        table = jnp.where((row == owner) & (col == rank), lax.rem(stored, 16), table)
    return table.reshape(8, 1, 128)


def start_fetch(me, req_ref, lib_ref, loads, asked, asked_s, stage, slots, table_sems, tile_sems):
    mine = me["x"] * 2 + me["c"]
    tables = []
    for n, (dx, dc) in enumerate(LIB_PEERS):
        at = lib_peer(me, dx, dc)
        cp = pltpu.make_async_remote_copy(
            src_ref=req_ref.at[at["x"] * 2 + at["c"]],
            dst_ref=asked.at[mine],
            send_sem=table_sems.at[0, n],
            recv_sem=table_sems.at[1, n],
            device_id=device_of(at),
            device_id_type=MESH,
        )
        cp.start()
        tables.append(cp)
    asked[mine] = req_ref[mine]
    for cp in tables:
        cp.wait_recv()
    local = pltpu.make_async_copy(asked, asked_s, table_sems.at[0, 7])
    local.start()
    local.wait()
    loads[0].wait()
    own_box = (lax.div(mine, 4), lax.rem(mine, 4))
    waves = []
    for k in range(CAP):
        wave = []
        for n, (dx, dc) in enumerate(LIB_PEERS):
            cp = pltpu.make_async_remote_copy(
                src_ref=stage.at[n // 4, n % 4, k],
                dst_ref=slots.at[own_box[0], own_box[1], k],
                send_sem=tile_sems.at[0, n * CAP + k],
                recv_sem=tile_sems.at[1, n * CAP + k],
                device_id=device_of(lib_peer(me, dx, dc)),
                device_id_type=MESH,
            )
            wave.append(cp)
        waves.append(wave)

    def stage_tile(n, k):
        at = lib_peer(me, *LIB_PEERS[n])
        peer = at["x"] * 2 + at["c"]
        stage[n // 4, n % 4, k] = lib_ref[asked_s[peer, 0, k]]

    for n in range(len(LIB_PEERS)):
        stage_tile(n, 0)
        waves[0][n].start()
    for k in range(1, CAP):
        for n in range(len(LIB_PEERS)):
            stage_tile(n, k)
    for cp in loads[1:]:
        cp.start()
    for k in range(CAP):
        slots[own_box[0], own_box[1], k] = lib_ref[asked_s[mine, 0, k]]
    return tables, waves


def w_part(ref, j):
    return ref.at[pl.ds(2 * j, 2)]


def step_kernel(
    x_hbm, g_hbm, gain_ref, w_hbm, lib_hbm, wanted, home,
    out_hbm, grad_hbm, wsum_ref, gsum_ref,
    req_ref, order_ref, g_ref, w_ref, lib_ref, load_sems,
    inv_ref, q_ref, dm_ref, mixed_ref, dsh_ref, kvs, tt_ref, at_ref, stage, slots,
    asked, asked_s, table_sems, tile_sems, gslots, gsend, grecv, pair_sems, free_sem,
    store_sems, *piece_bufs,
):
    me = my_coords()
    pairs = [(lib_hbm, lib_ref), (x_hbm, dsh_ref), (w_part(w_hbm, 0), w_part(w_ref, 0)), (g_hbm, g_ref)]
    pairs += [(w_part(w_hbm, j), w_part(w_ref, j)) for j in (3, 1, 2)]
    loads = [pltpu.make_async_copy(a, b, load_sems.at[n]) for n, (a, b) in enumerate(pairs)]
    loads[0].start()

    barrier = pltpu.get_barrier_semaphore()
    peers = [lib_peer(me, dx, dc) for dx, dc in LIB_PEERS]
    peers += [{**me, a: along(me, a, s)} for a in ("y", "z") for s in (1, 2, 3)]
    for at in peers:
        pl.semaphore_signal(barrier, inc=1, device_id=device_of(at), device_id_type=MESH)
    req_ref[...] = request_table(wanted, home, order_ref)
    pl.semaphore_wait(barrier, len(peers))

    tables, waves = start_fetch(
        me, req_ref, lib_ref, loads, asked, asked_s, stage, slots, table_sems, tile_sems
    )

    def matrix(j):
        return w_part(w_ref, j)[...].reshape(D, D)

    for cp in loads[1:5]:
        cp.wait()

    @pl.loop(0, 2)
    def _(s):
        rows = pl.ds(pl.multiple_of(s * SEQ, SEQ), SEQ)
        x = dsh_ref[rows].astype(F32)
        inv = lax.rsqrt(jnp.mean(x * x, axis=1, keepdims=True) + EPSILON)
        inv_ref[rows] = inv
        normed = (x * inv * gain_ref[...]).astype(BF16)
        at_ref[0, :, rows] = normed.T
        q_ref[rows] = shift_up_rows(dot(normed, matrix(0))).astype(BF16)
        dm_ref[rows] = shift_up_rows(dot(g_ref[rows], matrix(3), ((1,), (1,)))).astype(BF16)

    for cp in loads[5:]:
        cp.wait()

    for k in range(CAP):
        for n in range(len(LIB_PEERS)):
            waves[k][n].wait_send()
            if k + 1 < CAP:
                waves[k + 1][n].start()
        for dx in (0, 1):
            for n, (px, _) in enumerate(LIB_PEERS):
                if px % 2 == dx:
                    waves[k][n].wait_recv()
            chips = [along(me, "x", dx), along(me, "x", dx + 2)]
            t = [slots[lax.div(c, 2), pl.ds(lax.rem(c, 2) * 2, 2), k] for c in chips]
            t = jnp.concatenate([a.reshape(256, D) for a in t], axis=0)
            for half in range(2):
                c = slice(half * 512, half * 512 + 512)
                for m in range(2):
                    w = w_part(w_ref, 1 + m)[:, :, :, :, c].reshape(D, 512)
                    rows = dot(t, w).astype(BF16)
                    for o in range(4):
                        tile = rows[o * 128 : o * 128 + 128].reshape(4, 32, 512)
                        kvs[m, (chips[o // 2] * 2 + o % 2) * CAP + k, :, :, c] = tile

    pl.semaphore_signal(free_sem, inc=1, device_id=moved(me, "c", 1), device_id_type=MESH)

    @pl.loop(0, 16)
    def _(i):
        o = order_ref[i]
        t = slots[lax.div(o, 16), lax.rem(lax.div(o, 4), 4), lax.rem(o, 4)].reshape(128, D)
        tt_ref[:, pl.ds(pl.multiple_of(i * 128, 128), 128)] = t.T

    @pl.loop(0, 8, unroll=2)
    def _(b):
        attend(b, order_ref, q_ref, kvs.at[0], kvs.at[1], lib_ref, mixed_ref)

    @pl.loop(0, 2)
    def _(s):
        rows = pl.ds(pl.multiple_of(s * SEQ, SEQ), SEQ)
        attn = shift_down_rows(mixed_ref[rows].astype(F32)).astype(BF16)
        mixed_ref[rows] = attn
        at_ref[1, :, rows] = attn.T

    for cp in tables:
        cp.wait_send()

    sent = []
    pair = {}
    paired = w_ref.at[pl.ds(2, 4)]

    def weight_terms(p):
        cols = slice(p * 256, p * 256 + 256)
        pair[p] = []
        for j in (1, 2, 0, 3):
            for z in range(4):
                rows = slice(z * 256, z * 256 + 256)
                if j == 0:
                    res = dot(at_ref[0, rows, :], dsh_ref[:, cols])
                elif j == 3:
                    res = dot(at_ref[1, rows, :], g_ref[:, cols])
                else:
                    res = dot(tt_ref[rows, :], slots[j - 1, :, :, :, :, cols].reshape(2048, 256))
                res = res.astype(BF16)
                for xi in range(4):
                    for ci in range(2):
                        r0 = (xi * 2 + ci) * 32
                        stage[ci, j, z, xi, :, cols] = res[r0 : r0 + 32]
            if p == 0 and not pair[p]:
                pl.semaphore_wait(free_sem, 1)
            cp = start_pair(me, p, j, stage, paired, pair_sems)
            sent.append(cp)
            pair[p].append((j, cp))
            if p == PARTS - 1 and len(pair[p]) > 1:
                end_pair(me, p, stage, paired, pair[p][-2:-1])

    def back(g):
        @pl.loop(0, 2)
        def _(b):
            attend_back(
                b * 4, 4, g, order_ref, q_ref, dm_ref, kvs.at[0], kvs.at[1], lib_ref, slots, dsh_ref
            )

        for s in range(2):
            at = (pl.ds(s * SEQ, SEQ), slice(g * 256, g * 256 + 256))
            dsh_ref[at] = shift_down_rows(dsh_ref[at].astype(F32)).astype(BF16)

    stores = []

    def store(src, dst, rows):
        n = len(stores)
        stores.append(pltpu.make_async_copy(src.at[rows], dst.at[rows], store_sems.at[n]))
        stores[n].start()

    def out_rows(s):
        rows = pl.ds(s * SEQ, SEQ)
        x = q_ref[rows].astype(F32)
        mixed_ref[rows] = (x + dot(mixed_ref[rows], matrix(3))).astype(BF16)
        store(mixed_ref, out_hbm, rows)

    def grad_rows(s):
        rows = pl.ds(s * SEQ, SEQ)
        x = q_ref[rows].astype(F32)
        inv = inv_ref[rows]
        dn = dot(dsh_ref[rows], matrix(0), ((1,), (1,)))
        dnx = dn * x * inv
        term = jnp.sum(dnx, axis=0, keepdims=True)
        gslots[0] = term if s == 0 else gslots[0] + term
        dh = dn * gain_ref[...]
        inner = jnp.mean(dh * x, axis=1, keepdims=True)
        dx = inv * dh - x * (inv * inv * inv) * inner
        dsh_ref[rows] = (g_ref[rows].astype(F32) + dx).astype(BF16)
        store(dsh_ref, grad_hbm, rows)

    n_each = len(piece_bufs) // (2 * PARTS)
    flow = {}

    def sum_part(p):
        end_pair(me, p, stage, paired, pair[p][-1:] if p == PARTS - 1 else pair[p])
        flow[p] = []
        for h in range(2):
            q = 2 * p + h
            bufs = piece_bufs[q * n_each : (q + 1) * n_each]
            data = paired.at[:, :, :, :, pl.ds(q * 128, 128)]
            flow[p].append(reduce_piece(me, q, data, bufs, wsum_ref, sent))
            next(flow[p][-1])

    def advance(p):
        for f in flow[p]:
            next(f, None)

    back(0)
    weight_terms(0)
    back(1)
    sum_part(0)
    weight_terms(1)
    back(2)
    sum_part(1)
    advance(0)
    weight_terms(2)
    back(3)
    x_again = pltpu.make_async_copy(x_hbm, q_ref, load_sems.at[7])
    x_again.start()
    sum_part(2)
    advance(1)
    advance(0)
    weight_terms(3)
    x_again.wait()
    out_rows(0)
    sum_part(3)
    grad_rows(0)
    grad_rows(1)
    gain_flow = reduce_gain(me, gslots, gsend, grecv, sent)
    next(gain_flow)
    advance(2)
    advance(1)
    advance(0)
    out_rows(1)
    advance(3)
    next(gain_flow)
    advance(2)
    advance(1)
    advance(3)
    next(gain_flow)
    advance(2)
    advance(3)
    next(gain_flow, None)
    for cp in sent:
        cp.wait_send()
    for cp in stores:
        cp.wait()
    index = lax.axis_index("dp") * 8 + lax.axis_index("lib")
    gsum_ref[...] = pltpu.roll(gslots[0], lax.rem(D - index * 8, D), 1)[:, :128]


def train_step(hidden, cot, gains, weights, library, neighbours, tile_home):
    rows5 = (2, 4, 4, 4, 32, D)
    scratch = [
        pltpu.VMEM((8, 1, 128), jnp.int32),
        pltpu.SMEM((16,), jnp.int32),
        pltpu.VMEM((512, D), BF16),
        pltpu.VMEM((8, 4, 4, 32, D), BF16),
        pltpu.VMEM((16, 4, 32, D), BF16),
        pltpu.SemaphoreType.DMA((8,)),
        pltpu.VMEM((512, 1), F32),
        pltpu.VMEM((512, D), BF16),
        pltpu.VMEM((512, D), BF16),
        pltpu.VMEM((512, D), BF16),
        pltpu.VMEM((512, D), BF16),
        pltpu.VMEM((2, 32, 4, 32, D), BF16),
        pltpu.VMEM((D, 2048), BF16),
        pltpu.VMEM((2, D, 512), BF16),
        pltpu.VMEM(rows5, BF16),
        pltpu.VMEM(rows5, BF16),
        pltpu.VMEM((8, 1, 128), jnp.int32),
        pltpu.SMEM((8, 1, 128), jnp.int32),
        pltpu.SemaphoreType.DMA((2, 8)),
        pltpu.SemaphoreType.DMA((2, 28)),
        pltpu.VMEM((17, 1, D), F32),
        pltpu.SemaphoreType.DMA((13,)),
        pltpu.SemaphoreType.DMA((13,)),
        pltpu.SemaphoreType.DMA((2, 4 * PARTS)),
        pltpu.SemaphoreType.REGULAR,
        pltpu.SemaphoreType.DMA((4,)),
    ]
    for _ in range(2 * PARTS):
        scratch += piece_scratch()
    hbm = pl.BlockSpec(memory_space=pl.ANY)
    smem = pl.BlockSpec(memory_space=pltpu.SMEM)
    vmem = pl.BlockSpec(memory_space=pltpu.VMEM)
    return pl.pallas_call(
        step_kernel,
        out_shape=(
            jax.ShapeDtypeStruct((512, D), BF16),
            jax.ShapeDtypeStruct((512, D), BF16),
            jax.ShapeDtypeStruct((32, D), F32),
            jax.ShapeDtypeStruct((1, 128), F32),
        ),
        in_specs=[hbm, hbm, vmem, hbm, hbm, smem, smem],
        out_specs=(hbm, hbm, vmem, vmem),
        scratch_shapes=scratch,
        compiler_params=pltpu.CompilerParams(
            collective_id=1, has_side_effects=True, vmem_limit_bytes=67000000
        ),
        name="train_step",
    )(hidden, cot, gains, weights.reshape(8, 4, 4, 32, D), library.reshape(16, 4, 32, D), neighbours.T, tile_home)


def hand_over_kernel(out_in, grad_in, w_in, g_in, out_ref, grad_ref, w_ref, g_ref, sems):
    copies = []
    for src, dst, n in ((out_in, out_ref, 4), (grad_in, grad_ref, 4), (w_in, w_ref, 1)):
        rows = src.shape[0] // n
        for k in range(n):
            part = pl.ds(k * rows, rows)
            copies.append(
                pltpu.make_async_copy(src.at[part], dst.at[part], sems.at[len(copies)])
            )
            copies[-1].start()
    g_ref[...] = g_in[0, :8]
    for cp in copies:
        cp.wait()


def hand_over(out, grad, w_share, g_sum):
    hbm = pl.BlockSpec(memory_space=pl.ANY)
    vmem = pl.BlockSpec(memory_space=pltpu.VMEM)
    return pl.pallas_call(
        hand_over_kernel,
        out_shape=(
            jax.ShapeDtypeStruct(out.shape, out.dtype),
            jax.ShapeDtypeStruct(grad.shape, grad.dtype),
            jax.ShapeDtypeStruct(w_share.shape, w_share.dtype),
            jax.ShapeDtypeStruct((8,), F32),
        ),
        in_specs=[vmem] * 4,
        out_specs=(hbm, hbm, hbm, vmem),
        scratch_shapes=[pltpu.SemaphoreType.DMA((9,))],
        name="hand_over",
    )(out, grad, w_share, g_sum)


def body(hidden_in, cotangent, gains, weights, library, neighbours, tile_home):
    results = train_step(
        hidden_in, cotangent, gains, weights[0], library, neighbours, tile_home
    )
    return hand_over(*results)


def solution(mesh):
    return jax.shard_map(
        body,
        mesh=mesh,
        in_specs=(
            P(("dp", "lib"), None),
            P(("dp", "lib"), None),
            P(),
            P(),
            P(("dp", "lib"), None, None),
            P(("dp", "lib"), None),
            P("dp", None),
        ),
        out_specs=(
            P(("dp", "lib"), None),
            P(("dp", "lib"), None),
            P(("dp", "lib"), None),
            P(("dp", "lib")),
        ),
        check_vma=False,
    )
```
